32 devices in a mesh: grp: 2 (over x), node: 16 (over z, y, core).
Axes of the slice: x: 2, y: 2, z: 4, core: 2. Of those that a mesh axis runs over, the one named last changes fastest.
Arguments:
- blocks: float32 [3072, 128, 128], P(('grp', 'node')), parts along dimension 0, may hold values from 0.001 to 0.03
- block_row: int32 [3072], P(('grp', 'node')), parts along dimension 0, may hold values from 0 to 127, as said below
- block_patch: int32 [3072], P(('grp', 'node')), parts along dimension 0, may hold values from 0 to 7
- block_count: int32 [32], P(('grp', 'node')), parts along dimension 0, may hold values from 48 to 96, as said below
- row_map: int32 [256], P('grp'), parts along dimension 0, may hold values from 0 to 127, as said below
- sinogram: float32 [8, 16384], P('grp', 'node'), parts along dimension 0, may hold values from -96 to 96
- start: float32 [8, 16384], P('grp', 'node'), parts along dimension 0, may hold values from -6 to 6
Outputs:
- image: float32 [8, 16384], P('grp', 'node'), parts along dimension 0
- weighted: float32 [8, 16384], P('grp', 'node'), parts along dimension 0
The draws below stay inside these ranges and needn't reach their ends.
There are 2 independent parts, one for each index of `grp`. The reference program is written for one: setup_inputs(seed, part) draws one part's arguments, and reference() takes and returns one part's arrays. A program takes and returns all parts, laid end to end along the dimension named above; each array names one. Nothing has to cross between parts.
Inputs may be any that keep to these rules, and one draw needn't show every extreme that they name: `block_row`: of the 96 slots of one device, at most 6 have rows whose sinogram positions lie in one device's range (8 e to 8 e + 7); in every draw some device's range receives exactly 6 slots from every device. Slots from block_count on of a device are not part of the matrix; some device uses all 96. `row_map`: A permutation of the row blocks.
All inputs are finite; a program needn't handle non-finite values.
Results may differ from the reference program's by a relative error of at most 0.0001.
Values sent between devices are 32-bit elements; how exact they have to be, the bound alone decides.
No kernel may reach another device: no remote copies, remote signals or barrier semaphores. Data moves between devices by JAX's collectives and lax.ppermute only.
A program may use at most 64 MiB of HBM per device.

```python
import math
import jax
import jax.numpy as jnp
from jax import lax

BLK = 128
S = 4
NB = 96
RB = 8
PP = 8
ITERS = 2
NBLK = 1536
NR = 128
NP = 128
N_NODE = 16


def shared_layout(key):
    placing = jax.random.permutation(jax.random.fold_in(key, 11), NR).astype(jnp.int32)
    inverse = jnp.argsort(placing, stable=True).astype(jnp.int32)
    anchor_perm = jax.random.permutation(jax.random.fold_in(key, 12), N_NODE).astype(jnp.int32)
    half_pairs = NB // 2
    spare_room = half_pairs - N_NODE * ((half_pairs - 1) // N_NODE)
    offset = jax.random.randint(jax.random.fold_in(key, 13), (N_NODE,), 0, spare_room).astype(jnp.int32)
    pair_index = jnp.arange(NB, dtype=jnp.int32) // 2
    target = anchor_perm[(pair_index[None, :] - offset[:, None]) % N_NODE]
    within = jax.random.randint(jax.random.fold_in(key, 14), (N_NODE, NB), 0, RB).astype(jnp.int32)
    block_rows = inverse[target * RB + within].reshape(-1).astype(jnp.int32)
    return (placing, block_rows)


def draw_block_row(key, part):
    return shared_layout(key)[1]


def draw_row_map(key, part):
    return shared_layout(key)[0]


def draw_block_count(key, part):
    counts = jax.random.randint(jax.random.fold_in(key, 21), (N_NODE,), NB // 2, NB + 1).astype(jnp.int32)
    chosen = jax.random.randint(jax.random.fold_in(key, 22), (), 0, N_NODE).astype(jnp.int32)
    return jnp.where(jnp.arange(N_NODE, dtype=jnp.int32) == chosen, NB, counts).astype(jnp.int32)


def draw_blocks(key, part):
    key = jax.random.fold_in(key, 31)
    row_scale = jnp.exp(jax.random.uniform(jax.random.fold_in(key, 1), (NBLK, BLK, 1), jnp.float32, -1.7, 1.7))
    base = jnp.exp(jax.random.uniform(jax.random.fold_in(key, 2), (NBLK, BLK, BLK), jnp.float32, math.log(0.001), math.log(0.03)))
    return jnp.clip(base * row_scale, 0.001, 0.03).astype(jnp.float32)


def touch_ends(drawn, own_key, smallest, top_value):
    extent = drawn.shape
    spot = [jax.random.randint(jax.random.fold_in(own_key, axis), (), 0, extent[axis]) for axis in range(len(extent))]
    drawn = drawn.at[tuple(spot)].set(smallest)
    longest = extent.index(max(extent))
    spot[longest] = (spot[longest] + 1) % extent[longest]
    return drawn.at[tuple(spot)].set(top_value)


def level_of(key, shape, cuts, smallest, largest):
    gain = 1.0
    for dim, shards_of in cuts:
        draws = jax.random.uniform(jax.random.fold_in(jax.random.fold_in(key, 6), dim), (shards_of,), jnp.float32, smallest / len(cuts), largest / len(cuts))
        gain = gain * jnp.repeat(jnp.exp(draws), shape[dim] // shards_of).reshape((-1,) + (1,) * (len(shape) - 1 - dim))
    return gain


def normal_values(stream_key, dims, deviation, limit, split=(), kind=jnp.bfloat16):
    drawn = deviation * jax.random.normal(stream_key, dims, jnp.float32)
    if split:
        drawn = drawn * level_of(stream_key, dims, split, -0.22, 0.18)
    return jnp.clip(drawn, -limit, limit).astype(kind)


def setup_inputs(seed: int = 0, part: int = 0) -> dict:
    seeds = jax.random.split(jax.random.key(seed), 8)
    part_splits = jax.random.split(jax.random.fold_in(seeds[7], part), 8)
    blocks = draw_blocks(jax.random.fold_in(jax.random.fold_in(seeds[7], part), 71), part)
    block_row = draw_block_row(jax.random.fold_in(jax.random.fold_in(seeds[7], part), 71), part)
    block_patch = touch_ends(jax.random.randint(part_splits[2], (NBLK,), 0, PP), jax.random.fold_in(part_splits[2], 1), 0, PP - 1).astype(jnp.int32)
    block_count = draw_block_count(jax.random.fold_in(jax.random.fold_in(seeds[7], part), 71), part)
    row_map = draw_row_map(jax.random.fold_in(jax.random.fold_in(seeds[7], part), 71), part)
    sinogram = normal_values(part_splits[5], (S, NR * BLK), 16.0, 96.0, ((1, 16),), jnp.float32)
    start = normal_values(part_splits[6], (S, NP * BLK), 1.0, 6.0, ((1, 16),), jnp.float32)
    return {"blocks": blocks, "block_row": block_row, "block_patch": block_patch, "block_count": block_count, "row_map": row_map, "sinogram": sinogram, "start": start}


relax_factor = 1.9


def reference(blocks, block_row, block_patch, block_count, row_map, sinogram, start):
    total = blocks.shape[0]
    slot_index = jnp.arange(total, dtype=jnp.int32)
    holder = slot_index // NB
    live = (slot_index % NB < block_count[holder]).astype(jnp.float32)
    position = row_map[block_row].astype(jnp.int32)
    patch_index = (holder * PP + block_patch).astype(jnp.int32)
    row_totals = jax.ops.segment_sum(jnp.sum(blocks, axis=2) * live[:, None], position, num_segments=NR)
    col_totals = jax.ops.segment_sum(jnp.sum(blocks, axis=1) * live[:, None], patch_index, num_segments=NP)
    row_weight = 1.0 / (row_totals + 1.0)
    col_weight = 1.0 / (col_totals + 1.0)
    image = start.reshape(S, NP, BLK)
    measured = sinogram.reshape(S, NR, BLK)
    weighted = measured
    for sweep_index in range(ITERS):
        pieces = jnp.take(image, patch_index, axis=1)
        partial_value = jnp.einsum("sjc,jrc->jsr", pieces, blocks, precision=lax.Precision.HIGHEST) * live[:, None, None]
        projected = jax.ops.segment_sum(partial_value, position, num_segments=NR)
        weighted = row_weight[None] * (measured - jnp.transpose(projected, (1, 0, 2)))
        fetched = jnp.take(weighted, position, axis=1)
        back = jnp.einsum("sjr,jrc->jsc", fetched, blocks, precision=lax.Precision.HIGHEST) * live[:, None, None]
        summed = jax.ops.segment_sum(back, patch_index, num_segments=NP)
        image = image + relax_factor * col_weight[None] * jnp.transpose(summed, (1, 0, 2))
    return image.reshape(S, NP * BLK), weighted.reshape(S, NR * BLK)
```

```python
import functools

import jax
import jax.numpy as jnp
from jax import lax
from jax.experimental import pallas as pl
from jax.experimental.pallas import tpu as pltpu
from jax.sharding import PartitionSpec as P

ITERS = 2
CHUNKS = 8
GROUP = 8

relax_factor = 1.9

f32 = jnp.float32
bf16 = jnp.bfloat16


def split(value):
    high = value.astype(bf16).astype(f32)
    return high, value - high


def forward_terms(lhs_of, pair_of, slots):
    terms = []
    for j in slots:
        both = lax.dot_general(
            lhs_of(j).astype(bf16),
            pair_of(j),
            (((1,), (1,)), ((), ())),
            preferred_element_type=f32,
        )
        width = both.shape[1] // 2
        terms.append(both[:, :width] + both[:, width:])
    return terms


def backward_terms(lhs_of, pair_of, slots):
    terms = []
    for j in slots:
        lhs = lhs_of(j).astype(bf16)
        terms.append(
            jnp.dot(
                jnp.concatenate([lhs, lhs], axis=1),
                pair_of(j),
                preferred_element_type=f32,
            )
        )
    return terms


def at8(index):
    return pl.ds(pl.multiple_of(index * 8, 8), 8)


def first_kernel(
    slices,
    rows_ref,
    patch_ref,
    count_ref,
    map_ref,
    blocks_ref,
    start_ref,
    sino_ref,
    mine_ref,
    other_ref,
    col_ref,
    pair_ref,
    stage,
    lhs,
    acc,
    sums,
    cols,
    sems,
):
    count_blocks, width, _ = blocks_ref.shape
    total_rows = map_ref.shape[0]
    half = total_rows // 2
    patches = start_ref.shape[1] // width
    own = sino_ref.shape[1] // width
    node = lax.axis_index("node")
    core = lax.rem(node, 2)
    step = count_blocks // CHUNKS

    def copy(k):
        part = pl.ds(k * step, step)
        return pltpu.make_async_copy(blocks_ref.at[part], stage.at[part], sems.at[k])

    for k in range(CHUNKS):
        copy(k).start()
    acc[...] = jnp.zeros_like(acc)
    sums[...] = jnp.zeros_like(sums)
    cols[...] = jnp.zeros_like(cols)
    lhs[...] = jnp.zeros_like(lhs)
    for p in range(patches):
        high, low = split(start_ref[:, p * width : (p + 1) * width])
        lhs[p * 16 : p * 16 + slices, :] = high
        lhs[p * 16 + slices : p * 16 + 2 * slices, :] = low
        lhs[p * 16 + 8 : p * 16 + 9, :] = jnp.ones((1, width), f32)
    for r in range(own):
        acc[pl.ds((node * own + r) * 8, slices), :] = -sino_ref[:, r * width : (r + 1) * width]

    count = count_ref[0]

    def visit(base, size):
        slots = [base + i for i in range(size)]
        for j in slots:
            block = stage[j]
            block = jnp.where(j < count, block, 0.0)
            high = block.astype(bf16)
            pair_ref[j, :width, :] = high
            pair_ref[j, width:, :] = (block - high.astype(f32)).astype(bf16)
            part = jnp.sum(block.reshape(width // 8, 8, width), axis=0)
            cols[at8(patch_ref[j]), :] += part
        terms = forward_terms(
            lambda j: lhs[pl.ds(pl.multiple_of(patch_ref[j] * 16, 16), 16), :],
            lambda j: pair_ref[j],
            slots,
        )
        for j, term in zip(slots, terms):
            place = at8(map_ref[rows_ref[j]])
            acc[place, :] += term[:8]
            sums[place, :] += term[8:]

    for k in range(CHUNKS):
        copy(k).wait()
        size = min(GROUP, step)

        @pl.loop(0, step // size)
        def _(i):
            visit(k * step + i * size, size)

        for rest in range(step // size * size, step):
            visit(k * step + rest, 1)

    for ref, side in ((mine_ref, core), (other_ref, 1 - core)):
        base = side * half * 8
        for s in range(slices):
            ref[s] = (
                acc[pl.ds(base + s, half, stride=8), :]
                + acc[pl.ds(base + s + slices, half, stride=8), :]
            )
        ref[slices] = sums[pl.ds(base, half, stride=8), :]
    for p in range(patches):
        total = jnp.sum(cols[p * 8 : (p + 1) * 8, :], axis=0, keepdims=True)
        col_ref[p : p + 1, :] = relax_factor / (total + 1.0)


def weigh(slices, mine_ref, other_ref, weight_of, lhs, full, core, half):
    for ref, side in ((mine_ref, core), (other_ref, 1 - core)):
        weight = weight_of(ref, side)
        for s in range(slices):
            value = -weight * ref[s]
            high, low = split(value)
            lhs[pl.ds(side * half * 8 + s, half, stride=8), :] = high
            lhs[pl.ds(side * half * 8 + slices + s, half, stride=8), :] = low
            if full is not None:
                full[s, pl.ds(pl.multiple_of(side * half, 8), half), :] = value


def back_loop(count_blocks, rows_ref, patch_ref, map_ref, pair_ref, lhs, update):
    update[...] = jnp.zeros_like(update)

    @pl.loop(0, count_blocks // GROUP)
    def _(i):
        slots = [i * GROUP + g for g in range(GROUP)]
        terms = backward_terms(
            lambda j: lhs[at8(map_ref[rows_ref[j]]), :], lambda j: pair_ref[j], slots
        )
        for j, term in zip(slots, terms):
            update[at8(patch_ref[j]), :] += term


def middle_kernel(
    slices,
    rows_ref,
    patch_ref,
    map_ref,
    pair_ref,
    mine_ref,
    other_ref,
    col_ref,
    start_ref,
    sino_ref,
    next_mine_ref,
    next_other_ref,
    weight_ref,
    image_ref,
    lhs,
    update,
    acc,
    image_lhs,
):
    count_blocks, _, width = pair_ref.shape
    total_rows = map_ref.shape[0]
    half = total_rows // 2
    patches = start_ref.shape[1] // width
    own = sino_ref.shape[1] // width
    node = lax.axis_index("node")
    core = lax.rem(node, 2)

    def weight_of(ref, side):
        weight = 1.0 / (ref[slices] + 1.0)
        weight_ref[pl.ds(pl.multiple_of(side * half, 8), half), :] = weight
        return weight

    weigh(slices, mine_ref, other_ref, weight_of, lhs, None, core, half)
    back_loop(count_blocks, rows_ref, patch_ref, map_ref, pair_ref, lhs, update)
    for p in range(patches):
        total = update[p * 8 : p * 8 + slices, :] + update[p * 8 + slices : p * 8 + 2 * slices, :]
        value = start_ref[:, p * width : (p + 1) * width] + col_ref[p : p + 1, :] * total
        image_ref[:, p * width : (p + 1) * width] = value
        high, low = split(value)
        image_lhs[p * 8 : p * 8 + slices, :] = high
        image_lhs[p * 8 + slices : p * 8 + 2 * slices, :] = low
    acc[...] = jnp.zeros_like(acc)
    for r in range(own):
        acc[pl.ds((node * own + r) * 8, slices), :] = -sino_ref[:, r * width : (r + 1) * width]

    @pl.loop(0, count_blocks // GROUP)
    def _(i):
        slots = [i * GROUP + g for g in range(GROUP)]
        terms = forward_terms(
            lambda j: image_lhs[at8(patch_ref[j]), :], lambda j: pair_ref[j], slots
        )
        for j, term in zip(slots, terms):
            acc[at8(map_ref[rows_ref[j]]), :] += term

    for ref, side in ((next_mine_ref, core), (next_other_ref, 1 - core)):
        base = side * half * 8
        for s in range(slices):
            ref[s] = (
                acc[pl.ds(base + s, half, stride=8), :]
                + acc[pl.ds(base + s + slices, half, stride=8), :]
            )


def last_kernel(
    slices,
    rows_ref,
    patch_ref,
    map_ref,
    pair_ref,
    mine_ref,
    other_ref,
    col_ref,
    prior_ref,
    weight_ref,
    image_ref,
    weighted_ref,
    lhs,
    full,
    update,
):
    count_blocks, _, width = pair_ref.shape
    half = map_ref.shape[0] // 2
    patches = prior_ref.shape[1] // width
    own = weighted_ref.shape[1] // width
    node = lax.axis_index("node")
    core = lax.rem(node, 2)

    def weight_of(ref, side):
        return weight_ref[pl.ds(pl.multiple_of(side * half, 8), half), :]

    weigh(slices, mine_ref, other_ref, weight_of, lhs, full, core, half)
    back_loop(count_blocks, rows_ref, patch_ref, map_ref, pair_ref, lhs, update)
    for p in range(patches):
        total = update[p * 8 : p * 8 + slices, :] + update[p * 8 + slices : p * 8 + 2 * slices, :]
        image_ref[:, p * width : (p + 1) * width] = (
            prior_ref[:, p * width : (p + 1) * width] + col_ref[p : p + 1, :] * total
        )
    for s in range(slices):
        for r in range(own):
            weighted_ref[s : s + 1, r * width : (r + 1) * width] = full[
                s, pl.ds(node * own + r, 1), :
            ]


def exchange(value, distance, nodes):
    return lax.ppermute(value, "node", [(i, i ^ distance) for i in range(nodes)])


def body(blocks, block_row, block_patch, block_count, row_map, sinogram, start):
    nodes = lax.axis_size("node")
    count_blocks, width, _ = blocks.shape
    slices = start.shape[0]
    patches = start.shape[1] // width
    total_rows = row_map.shape[0]
    half = total_rows // 2
    smem = pl.BlockSpec(memory_space=pltpu.SMEM)
    vmem = pl.BlockSpec(memory_space=pltpu.VMEM)
    params = pltpu.CompilerParams(vmem_limit_bytes=32 * 1024 * 1024)

    def sum_over_nodes(mine, other):
        value = mine + exchange(other, 1, nodes)
        distance = 2
        while distance < nodes:
            value = value + exchange(value, distance, nodes)
            distance *= 2
        return value, exchange(value, 1, nodes)

    mine, other, col, pair = pl.pallas_call(
        functools.partial(first_kernel, slices),
        out_shape=(
            jax.ShapeDtypeStruct((slices + 1, half, width), f32),
            jax.ShapeDtypeStruct((slices + 1, half, width), f32),
            jax.ShapeDtypeStruct((patches, width), f32),
            pltpu.VMEM((count_blocks, 2 * width, width), bf16),
        ),
        in_specs=[smem] * 4 + [pl.BlockSpec(memory_space=pl.ANY), vmem, vmem],
        out_specs=(vmem,) * 4,
        scratch_shapes=[
            pltpu.VMEM(blocks.shape, f32),
            pltpu.VMEM((patches * 16, width), f32),
            pltpu.VMEM((total_rows * 8, width), f32),
            pltpu.VMEM((total_rows * 8, width), f32),
            pltpu.VMEM((patches * 8, width), f32),
            pltpu.SemaphoreType.DMA((CHUNKS,)),
        ],
        compiler_params=params,
        name="first",
    )(block_row, block_patch, block_count, row_map, blocks, start, sinogram)
    mine, other = sum_over_nodes(mine, other)
    held = pltpu.with_memory_space_constraint(pair, pltpu.VMEM)
    mine, other, weight, image = pl.pallas_call(
        functools.partial(middle_kernel, slices),
        out_shape=(
            jax.ShapeDtypeStruct((slices, half, width), f32),
            jax.ShapeDtypeStruct((slices, half, width), f32),
            jax.ShapeDtypeStruct((total_rows, width), f32),
            jax.ShapeDtypeStruct(start.shape, f32),
        ),
        in_specs=[smem] * 3 + [vmem] * 6,
        out_specs=(vmem,) * 4,
        scratch_shapes=[
            pltpu.VMEM((total_rows * 8, width), f32),
            pltpu.VMEM((patches * 8, width), f32),
            pltpu.VMEM((total_rows * 8, width), f32),
            pltpu.VMEM((patches * 8, width), f32),
        ],
        compiler_params=params,
        name="middle",
    )(block_row, block_patch, row_map, held, mine, other, col, start, sinogram)
    mine, other = sum_over_nodes(mine, other)
    held = pltpu.with_memory_space_constraint(pair, pltpu.VMEM)
    image, weighted = pl.pallas_call(
        functools.partial(last_kernel, slices),
        out_shape=(
            jax.ShapeDtypeStruct(start.shape, f32),
            jax.ShapeDtypeStruct(sinogram.shape, f32),
        ),
        in_specs=[smem] * 3 + [vmem] * 6,
        out_specs=(vmem,) * 2,
        scratch_shapes=[
            pltpu.VMEM((total_rows * 8, width), f32),
            pltpu.VMEM((slices, total_rows, width), f32),
            pltpu.VMEM((patches * 8, width), f32),
        ],
        compiler_params=params,
        name="last",
    )(block_row, block_patch, row_map, held, mine, other, col, image, weight)
    return image, weighted


def solution(mesh):
    placed = (
        P(("grp", "node"), None, None),
        P(("grp", "node")),
        P(("grp", "node")),
        P(("grp", "node")),
        P("grp"),
        P("grp", "node"),
        P("grp", "node"),
    )
    return jax.shard_map(
        body,
        mesh=mesh,
        in_specs=placed,
        out_specs=(P("grp", "node"), P("grp", "node")),
        check_vma=False,
    )
```

```python
import functools

import jax
import jax.numpy as jnp
from jax import lax
from jax.experimental import pallas as pl
from jax.experimental.pallas import tpu as pltpu
from jax.sharding import PartitionSpec as P

CHUNKS = 8
CHAINS = 1

relax_factor = 1.9

f32 = jnp.float32
bf16 = jnp.bfloat16


def split(value):
    high = value.astype(bf16).astype(f32)
    return high, value - high


def forward_term(lhs, pair):
    both = lax.dot_general(
        lhs.astype(bf16), pair, (((1,), (1,)), ((), ())), preferred_element_type=f32
    )
    width = both.shape[1] // 2
    return both[:, :width] + both[:, width:]


def backward_term(lhs, pair):
    lhs = lhs.astype(bf16)
    return jnp.dot(
        jnp.concatenate([lhs, lhs], axis=1), pair, preferred_element_type=f32
    )


def at8(index):
    return pl.ds(pl.multiple_of(index * 8, 8), 8)


def minus_measured(acc, sino_ref, width, node):
    own = sino_ref.shape[1] // width
    slices = sino_ref.shape[0]
    for r in range(own):
        acc[pl.ds((node * own + r) * 8, slices), :] = -sino_ref[:, r * width : (r + 1) * width]


def write_halves(acc, slices, core, half, mine_ref, other_ref):
    for ref, side in ((mine_ref, core), (other_ref, 1 - core)):
        base = side * half * 8
        for s in range(slices):
            ref[s] = (
                acc[pl.ds(base + s, half, stride=8), :]
                + acc[pl.ds(base + s + slices, half, stride=8), :]
            )


def fill_lhs(lhs, p, stride, value, slices):
    high, low = split(value)
    lhs[p * stride : p * stride + slices, :] = high
    lhs[p * stride + slices : p * stride + 2 * slices, :] = low


def first_kernel(
    lo,
    slices,
    rows_hbm,
    patch_hbm,
    count_ref,
    map_hbm,
    blocks_ref,
    start_hbm,
    sino_hbm,
    mine_ref,
    other_ref,
    col_ref,
    pair_ref,
    index_ref,
    rows_ref,
    patch_ref,
    map_ref,
    start_ref,
    sino_ref,
    stage,
    lhs,
    acc,
    sums,
    cols,
    sems,
    small_sems,
):
    count_blocks, width, _ = blocks_ref.shape
    total_rows = map_ref.shape[0]
    half = total_rows // 2
    patches = start_ref.shape[1] // width
    node = lax.axis_index("node")
    core = lax.rem(node, 2)
    step = count_blocks // CHUNKS

    def copy(k):
        part = pl.ds(k * step, step)
        return pltpu.make_async_copy(blocks_ref.at[part], stage.at[part], sems.at[k])

    small = [
        pltpu.make_async_copy(src, dst, small_sems.at[i])
        for i, (src, dst) in enumerate(
            (
                (start_hbm, start_ref),
                (sino_hbm, sino_ref),
                (rows_hbm, rows_ref),
                (patch_hbm, patch_ref),
                (map_hbm, map_ref),
            )
        )
    ]
    copy(0).start()
    for one in small:
        one.start()
    for k in range(1, CHUNKS):
        copy(k).start()
    acc[...] = jnp.zeros_like(acc)
    sums[...] = jnp.zeros_like(sums)
    cols[...] = jnp.zeros_like(cols)
    lhs[...] = jnp.zeros_like(lhs)
    for one in small:
        one.wait()
    for p in range(patches):
        fill_lhs(lhs, p, 16, start_ref[lo : lo + slices, p * width : (p + 1) * width], slices)
        lhs[p * 16 + 8 : p * 16 + 9, :] = jnp.ones((1, width), f32)
    minus_measured(acc, sino_ref.at[lo : lo + slices], width, node)
    count = count_ref[0]

    for k in range(CHUNKS):
        copy(k).wait()
        slots = range(k * step, (k + 1) * step)
        places = []
        terms = []
        for j in slots:
            position = map_ref[rows_ref[j]]
            patch = patch_ref[j]
            index_ref[0, j] = position
            index_ref[1, j] = patch
            places.append(at8(position))
            block = jnp.where(j < count, stage[j], 0.0)
            high = block.astype(bf16)
            pair = jnp.concatenate([high, (block - high.astype(f32)).astype(bf16)], axis=0)
            pair_ref[j] = pair
            cols[at8(patch), :] += jnp.sum(block.reshape(width // 8, 8, width), axis=0)
            terms.append(
                forward_term(lhs[pl.ds(pl.multiple_of(patch * 16, 16), 16), :], pair)
            )
        for place, term in zip(places, terms):
            acc[place, :] += term[:8]
            sums[place, :] += term[8:]

    write_halves(acc, slices, core, half, mine_ref, other_ref)
    for ref, side in ((mine_ref, core), (other_ref, 1 - core)):
        ref[slices] = sums[pl.ds(side * half * 8, half, stride=8), :]
    for p in range(patches):
        total = jnp.sum(cols[p * 8 : (p + 1) * 8, :], axis=0, keepdims=True)
        col_ref[p : p + 1, :] = relax_factor / (total + 1.0)


def weigh(slices, mine_ref, other_ref, weight_of, lhs, full, core, half):
    for ref, side in ((mine_ref, core), (other_ref, 1 - core)):
        weight = weight_of(ref, side)
        for s in range(slices):
            value = -weight * ref[s]
            high, low = split(value)
            lhs[pl.ds(side * half * 8 + s, half, stride=8), :] = high
            lhs[pl.ds(side * half * 8 + slices + s, half, stride=8), :] = low
            if full is not None:
                full[s, pl.ds(pl.multiple_of(side * half, 8), half), :] = value


def backward(index_ref, pair_ref, lhs, update):
    update[...] = jnp.zeros_like(update)
    terms = []
    for j in range(pair_ref.shape[0]):
        terms.append(backward_term(lhs[at8(index_ref[0, j]), :], pair_ref[j]))
    for j, term in enumerate(terms):
        update[at8(index_ref[1, j]), :] += term


def forward(index_ref, pair_ref, lhs, acc):
    terms = []
    for j in range(pair_ref.shape[0]):
        terms.append(forward_term(lhs[at8(index_ref[1, j]), :], pair_ref[j]))
    for j, term in enumerate(terms):
        acc[at8(index_ref[0, j]), :] += term


def second_kernel(
    lo, slices, index_ref, pair_ref, start_ref, sino_ref, mine_ref, other_ref, acc, image_lhs
):
    width = pair_ref.shape[2]
    half = mine_ref.shape[1]
    patches = start_ref.shape[1] // width
    node = lax.axis_index("node")
    image_lhs[...] = jnp.zeros_like(image_lhs)
    for p in range(patches):
        fill_lhs(image_lhs, p, 8, start_ref[lo : lo + slices, p * width : (p + 1) * width], slices)
    acc[...] = jnp.zeros_like(acc)
    minus_measured(acc, sino_ref.at[lo : lo + slices], width, node)
    forward(index_ref, pair_ref, image_lhs, acc)
    write_halves(acc, slices, lax.rem(node, 2), half, mine_ref, other_ref)


def middle_kernel(
    lo,
    slices,
    index_ref,
    pair_ref,
    mine_ref,
    other_ref,
    col_ref,
    start_ref,
    sino_ref,
    *rest,
):
    given, rest = (rest[:1], rest[1:]) if lo else ((), rest)
    next_mine_ref, next_other_ref, image_ref = rest[:3]
    made, rest = (rest[3:4], rest[4:]) if not lo else ((), rest[3:])
    lhs, update, acc, image_lhs = rest
    width = pair_ref.shape[2]
    half = mine_ref.shape[1]
    patches = start_ref.shape[1] // width
    node = lax.axis_index("node")
    core = lax.rem(node, 2)

    def weight_of(ref, side):
        part = pl.ds(pl.multiple_of(side * half, 8), half)
        if given:
            return given[0][part, :]
        weight = 1.0 / (ref[slices] + 1.0)
        made[0][part, :] = weight
        return weight

    if slices < 4:
        lhs[...] = jnp.zeros_like(lhs)
        image_lhs[...] = jnp.zeros_like(image_lhs)
    weigh(slices, mine_ref, other_ref, weight_of, lhs, None, core, half)
    backward(index_ref, pair_ref, lhs, update)
    for p in range(patches):
        total = update[p * 8 : p * 8 + slices, :] + update[p * 8 + slices : p * 8 + 2 * slices, :]
        value = (
            start_ref[lo : lo + slices, p * width : (p + 1) * width]
            + col_ref[p : p + 1, :] * total
        )
        image_ref[:, p * width : (p + 1) * width] = value
        fill_lhs(image_lhs, p, 8, value, slices)
    acc[...] = jnp.zeros_like(acc)
    minus_measured(acc, sino_ref.at[lo : lo + slices], width, node)
    forward(index_ref, pair_ref, image_lhs, acc)
    write_halves(acc, slices, core, half, next_mine_ref, next_other_ref)


def last_kernel(
    lo,
    slices,
    index_ref,
    pair_ref,
    mine_ref,
    other_ref,
    col_ref,
    prior_ref,
    weight_ref,
    *rest,
):
    earlier, rest = (rest[:2], rest[2:]) if lo else ((), rest)
    image_ref, weighted_ref, lhs, full, update = rest
    width = pair_ref.shape[2]
    half = mine_ref.shape[1]
    patches = prior_ref.shape[1] // width
    own = weighted_ref.shape[1] // width
    node = lax.axis_index("node")
    core = lax.rem(node, 2)

    def weight_of(ref, side):
        return weight_ref[pl.ds(pl.multiple_of(side * half, 8), half), :]

    if slices < 4:
        lhs[...] = jnp.zeros_like(lhs)
    if earlier:
        image_ref[:lo, :] = earlier[0][...]
        weighted_ref[:lo, :] = earlier[1][...]
    weigh(slices, mine_ref, other_ref, weight_of, lhs, full, core, half)
    for s in range(slices):
        for r in range(own):
            weighted_ref[lo + s : lo + s + 1, r * width : (r + 1) * width] = full[
                s, pl.ds(node * own + r, 1), :
            ]
    backward(index_ref, pair_ref, lhs, update)
    for p in range(patches):
        total = update[p * 8 : p * 8 + slices, :] + update[p * 8 + slices : p * 8 + 2 * slices, :]
        image_ref[lo : lo + slices, p * width : (p + 1) * width] = (
            prior_ref[:, p * width : (p + 1) * width] + col_ref[p : p + 1, :] * total
        )


def exchange(value, distance, nodes):
    return lax.ppermute(value, "node", [(i, i ^ distance) for i in range(nodes)])


def body(blocks, block_row, block_patch, block_count, row_map, sinogram, start):
    nodes = lax.axis_size("node")
    count_blocks, width, _ = blocks.shape
    all_slices, pixels = start.shape
    slices = all_slices // CHAINS
    patches = pixels // width
    total_rows = row_map.shape[0]
    half = total_rows // 2
    hbm = pl.BlockSpec(memory_space=pltpu.HBM)
    smem = pl.BlockSpec(memory_space=pltpu.SMEM)
    vmem = pl.BlockSpec(memory_space=pltpu.VMEM)
    params = pltpu.CompilerParams(vmem_limit_bytes=28 * 1024 * 1024)
    small_params = pltpu.CompilerParams(vmem_limit_bytes=20 * 1024 * 1024)

    def in_hbm(value):
        return pltpu.with_memory_space_constraint(value, pltpu.HBM)

    def array(*shape):
        return jax.ShapeDtypeStruct(shape, f32)

    def sum_over_nodes(mine, other):
        value = mine + exchange(other, 1, nodes)
        distance = 2
        while distance < nodes:
            value = value + exchange(value, distance, nodes)
            distance *= 2
        return value, exchange(value, 1, nodes)

    acc_shape = pltpu.VMEM((total_rows * 8, width), f32)
    patch_shape = pltpu.VMEM((patches * 8, width), f32)

    mine, other, col, pair, index = pl.pallas_call(
        functools.partial(first_kernel, 0, slices),
        out_shape=(
            array(slices + 1, half, width),
            array(slices + 1, half, width),
            array(patches, width),
            pltpu.VMEM((count_blocks, 2 * width, width), bf16),
            pltpu.SMEM((2, count_blocks), jnp.int32),
        ),
        in_specs=[hbm] * 2 + [smem] + [hbm] * 4,
        out_specs=(vmem,) * 4 + (smem,),
        scratch_shapes=[
            pltpu.SMEM(block_row.shape, jnp.int32),
            pltpu.SMEM(block_patch.shape, jnp.int32),
            pltpu.SMEM(row_map.shape, jnp.int32),
            pltpu.VMEM(start.shape, f32),
            pltpu.VMEM(sinogram.shape, f32),
            pltpu.VMEM(blocks.shape, f32),
            pltpu.VMEM((patches * 16, width), f32),
            acc_shape,
            acc_shape,
            patch_shape,
            pltpu.SemaphoreType.DMA((CHUNKS,)),
            pltpu.SemaphoreType.DMA((5,)),
        ],
        compiler_params=params,
        name="first",
    )(
        in_hbm(block_row),
        in_hbm(block_patch),
        block_count,
        *map(in_hbm, (row_map, blocks, start, sinogram)),
    )

    def held():
        return (
            pltpu.with_memory_space_constraint(index, pltpu.SMEM),
            pltpu.with_memory_space_constraint(pair, pltpu.VMEM),
        )

    terms = [(mine, other)]
    for chain in range(1, CHAINS):
        terms.append(
            pl.pallas_call(
                functools.partial(second_kernel, chain * slices, slices),
                out_shape=(array(slices, half, width),) * 2,
                in_specs=[smem] + [vmem] * 3,
                out_specs=(vmem,) * 2,
                scratch_shapes=[acc_shape, patch_shape],
                compiler_params=small_params,
                name="second",
            )(*held(), start, sinogram)
        )
    images = []
    weight = None
    for chain in range(CHAINS):
        given = (weight,) if chain else ()
        got = pl.pallas_call(
            functools.partial(middle_kernel, chain * slices, slices),
            out_shape=(
                array(slices, half, width),
                array(slices, half, width),
                array(slices, pixels),
            )
            + (() if chain else (array(total_rows, width),)),
            in_specs=[smem] + [vmem] * (6 + len(given)),
            out_specs=(vmem,) * (3 if chain else 4),
            scratch_shapes=[acc_shape, patch_shape, acc_shape, patch_shape],
            compiler_params=small_params,
            name="middle",
        )(*held(), *sum_over_nodes(*terms[chain]), col, start, sinogram, *given)
        terms[chain] = got[:2]
        images.append(got[2])
        if not chain:
            weight = got[3]
    results = ()
    for chain in range(CHAINS):
        upto = (chain + 1) * slices
        results = pl.pallas_call(
            functools.partial(last_kernel, chain * slices, slices),
            out_shape=(array(upto, pixels), array(upto, sinogram.shape[1])),
            in_specs=[smem] + [vmem] * (6 + len(results)),
            out_specs=(vmem,) * 2,
            scratch_shapes=[
                acc_shape,
                pltpu.VMEM((slices, total_rows, width), f32),
                patch_shape,
            ],
            compiler_params=small_params,
            name="last",
        )(*held(), *sum_over_nodes(*terms[chain]), col, images[chain], weight, *results)
    return results


def solution(mesh):
    placed = (
        P(("grp", "node"), None, None),
        P(("grp", "node")),
        P(("grp", "node")),
        P(("grp", "node")),
        P("grp"),
        P("grp", "node"),
        P("grp", "node"),
    )
    return jax.shard_map(
        body,
        mesh=mesh,
        in_specs=placed,
        out_specs=(P("grp", "node"), P("grp", "node")),
        check_vma=False,
    )
```

```python
import functools

import jax
import jax.numpy as jnp
from jax import lax
from jax.experimental import pallas as pl
from jax.experimental.pallas import tpu as pltpu
from jax.sharding import PartitionSpec as P

CHUNKS = 4
CHAINS = 1

relax_factor = 1.9

f32 = jnp.float32
bf16 = jnp.bfloat16


def split(value):
    high = value.astype(bf16).astype(f32)
    return high, value - high


def forward_term(lhs, pair):
    both = lax.dot_general(
        lhs.astype(bf16), pair, (((1,), (1,)), ((), ())), preferred_element_type=f32
    )
    width = both.shape[1] // 2
    return both[:, :width] + both[:, width:]


def backward_term(lhs, pair):
    lhs = lhs.astype(bf16)
    return jnp.dot(
        jnp.concatenate([lhs, lhs], axis=1), pair, preferred_element_type=f32
    )


def at8(index):
    return pl.ds(pl.multiple_of(index * 8, 8), 8)


def minus_measured(acc, sino_ref, lo, slices, width, node):
    own = sino_ref.shape[1] // width
    for r in range(own):
        acc[pl.ds((node * own + r) * 8, slices), :] = -sino_ref[
            lo : lo + slices, r * width : (r + 1) * width
        ]


def write_halves(acc, slices, core, half, mine_ref, other_ref):
    for ref, side in ((mine_ref, core), (other_ref, 1 - core)):
        base = side * half * 8
        for s in range(slices):
            ref[s] = (
                acc[pl.ds(base + s, half, stride=8), :]
                + acc[pl.ds(base + s + slices, half, stride=8), :]
            )


def fill_lhs(lhs, p, stride, value, slices):
    high, low = split(value)
    lhs[p * stride : p * stride + slices, :] = high
    lhs[p * stride + slices : p * stride + 2 * slices, :] = low


def first_kernel(
    lo,
    slices,
    rows_hbm,
    patch_hbm,
    count_hbm,
    map_hbm,
    blocks_ref,
    start_hbm,
    sino_hbm,
    mine_ref,
    other_ref,
    col_ref,
    pair_ref,
    index_ref,
    rows_ref,
    patch_ref,
    count_ref,
    map_ref,
    start_ref,
    sino_ref,
    stage,
    lhs,
    acc,
    sums,
    cols,
    sems,
    small_sems,
):
    count_blocks, width, _ = blocks_ref.shape
    total_rows = map_ref.shape[0]
    half = total_rows // 2
    patches = start_ref.shape[1] // width
    node = lax.axis_index("node")
    core = lax.rem(node, 2)
    step = count_blocks // CHUNKS

    def copy(k):
        part = pl.ds(k * step, step)
        return pltpu.make_async_copy(blocks_ref.at[part], stage.at[part], sems.at[k])

    small = [
        pltpu.make_async_copy(src, dst, small_sems.at[i])
        for i, (src, dst) in enumerate(
            (
                (start_hbm, start_ref),
                (sino_hbm, sino_ref),
                (rows_hbm, rows_ref),
                (patch_hbm, patch_ref),
                (count_hbm, count_ref),
                (map_hbm, map_ref),
            )
        )
    ]
    copy(0).start()
    for one in small:
        one.start()
    for k in range(1, CHUNKS):
        copy(k).start()
    acc[...] = jnp.zeros_like(acc)
    sums[...] = jnp.zeros_like(sums)
    cols[...] = jnp.zeros_like(cols)
    lhs[...] = jnp.zeros_like(lhs)
    for one in small:
        one.wait()
    for p in range(patches):
        fill_lhs(lhs, p, 16, start_ref[lo : lo + slices, p * width : (p + 1) * width], slices)
        lhs[p * 16 + 8 : p * 16 + 9, :] = jnp.ones((1, width), f32)
    minus_measured(acc, sino_ref, lo, slices, width, node)
    count = count_ref[0]

    for k in range(CHUNKS):
        copy(k).wait()
        slots = range(k * step, (k + 1) * step)
        places = []
        terms = []
        for j in slots:
            live = j < count
            position = jnp.where(live, map_ref[rows_ref[j]], total_rows)
            patch = jnp.where(live, patch_ref[j], patches)
            index_ref[0, j] = position
            index_ref[1, j] = patch
            places.append(at8(position))
            block = stage[j]
            high = block.astype(bf16)
            pair = jnp.concatenate([high, (block - high.astype(f32)).astype(bf16)], axis=0)
            pair_ref[j] = pair
            cols[at8(patch), :] += jnp.sum(block.reshape(width // 8, 8, width), axis=0)
            terms.append(
                forward_term(lhs[pl.ds(pl.multiple_of(patch * 16, 16), 16), :], pair)
            )
        for place, term in zip(places, terms):
            acc[place, :] += term[:8]
            sums[place, :] += term[8:]

    write_halves(acc, slices, core, half, mine_ref, other_ref)
    for ref, side in ((mine_ref, core), (other_ref, 1 - core)):
        ref[slices] = sums[pl.ds(side * half * 8, half, stride=8), :]
    for p in range(patches):
        total = jnp.sum(cols[p * 8 : (p + 1) * 8, :], axis=0, keepdims=True)
        col_ref[p : p + 1, :] = relax_factor / (total + 1.0)


def weigh(slices, mine_ref, other_ref, weight_of, lhs, full, core, half):
    for ref, side in ((mine_ref, core), (other_ref, 1 - core)):
        weight = weight_of(ref, side)
        for s in range(slices):
            value = -weight * ref[s]
            high, low = split(value)
            lhs[pl.ds(side * half * 8 + s, half, stride=8), :] = high
            lhs[pl.ds(side * half * 8 + slices + s, half, stride=8), :] = low
            if full is not None:
                full[s, pl.ds(pl.multiple_of(side * half, 8), half), :] = value


def backward(index_ref, pair_ref, lhs, update):
    update[...] = jnp.zeros_like(update)
    terms = []
    for j in range(pair_ref.shape[0]):
        terms.append(backward_term(lhs[at8(index_ref[0, j]), :], pair_ref[j]))
    for j, term in enumerate(terms):
        update[at8(index_ref[1, j]), :] += term


def forward(index_ref, pair_ref, lhs, acc):
    terms = []
    for j in range(pair_ref.shape[0]):
        terms.append(forward_term(lhs[at8(index_ref[1, j]), :], pair_ref[j]))
    for j, term in enumerate(terms):
        acc[at8(index_ref[0, j]), :] += term


def second_kernel(
    lo, slices, index_ref, pair_ref, start_ref, sino_ref, mine_ref, other_ref, acc, image_lhs
):
    width = pair_ref.shape[2]
    half = mine_ref.shape[1]
    patches = start_ref.shape[1] // width
    node = lax.axis_index("node")
    image_lhs[...] = jnp.zeros_like(image_lhs)
    for p in range(patches):
        fill_lhs(image_lhs, p, 8, start_ref[lo : lo + slices, p * width : (p + 1) * width], slices)
    acc[...] = jnp.zeros_like(acc)
    minus_measured(acc, sino_ref, lo, slices, width, node)
    forward(index_ref, pair_ref, image_lhs, acc)
    write_halves(acc, slices, lax.rem(node, 2), half, mine_ref, other_ref)


def middle_kernel(
    lo,
    slices,
    index_ref,
    pair_ref,
    mine_ref,
    other_ref,
    col_ref,
    start_ref,
    sino_ref,
    *rest,
):
    given, rest = (rest[:1], rest[1:]) if lo else ((), rest)
    next_mine_ref, next_other_ref, image_ref = rest[:3]
    made, rest = (rest[3:4], rest[4:]) if not lo else ((), rest[3:])
    lhs, update, acc, image_lhs = rest
    width = pair_ref.shape[2]
    half = mine_ref.shape[1]
    patches = start_ref.shape[1] // width
    node = lax.axis_index("node")
    core = lax.rem(node, 2)

    def weight_of(ref, side):
        part = pl.ds(pl.multiple_of(side * half, 8), half)
        if given:
            return given[0][part, :]
        weight = 1.0 / (ref[slices] + 1.0)
        made[0][part, :] = weight
        return weight

    if slices < 4:
        lhs[...] = jnp.zeros_like(lhs)
        image_lhs[...] = jnp.zeros_like(image_lhs)
    lhs[2 * half * 8 :, :] = jnp.zeros((8, width), f32)
    image_lhs[patches * 8 :, :] = jnp.zeros((8, width), f32)
    weigh(slices, mine_ref, other_ref, weight_of, lhs, None, core, half)
    backward(index_ref, pair_ref, lhs, update)
    for p in range(patches):
        total = update[p * 8 : p * 8 + slices, :] + update[p * 8 + slices : p * 8 + 2 * slices, :]
        value = (
            start_ref[lo : lo + slices, p * width : (p + 1) * width]
            + col_ref[p : p + 1, :] * total
        )
        image_ref[:, p * width : (p + 1) * width] = value
        fill_lhs(image_lhs, p, 8, value, slices)
    acc[...] = jnp.zeros_like(acc)
    minus_measured(acc, sino_ref, lo, slices, width, node)
    forward(index_ref, pair_ref, image_lhs, acc)
    write_halves(acc, slices, core, half, next_mine_ref, next_other_ref)


def last_kernel(
    lo,
    slices,
    index_ref,
    pair_ref,
    mine_ref,
    other_ref,
    col_ref,
    prior_ref,
    weight_ref,
    *rest,
):
    earlier, rest = (rest[:2], rest[2:]) if lo else ((), rest)
    image_ref, weighted_ref, lhs, full, update = rest
    width = pair_ref.shape[2]
    half = mine_ref.shape[1]
    patches = prior_ref.shape[1] // width
    own = weighted_ref.shape[1] // width
    node = lax.axis_index("node")
    core = lax.rem(node, 2)

    def weight_of(ref, side):
        return weight_ref[pl.ds(pl.multiple_of(side * half, 8), half), :]

    if slices < 4:
        lhs[...] = jnp.zeros_like(lhs)
    if earlier:
        image_ref[:lo, :] = earlier[0][...]
        weighted_ref[:lo, :] = earlier[1][...]
    lhs[2 * half * 8 :, :] = jnp.zeros((8, width), f32)
    weigh(slices, mine_ref, other_ref, weight_of, lhs, full, core, half)
    for s in range(slices):
        for r in range(own):
            weighted_ref[lo + s : lo + s + 1, r * width : (r + 1) * width] = full[
                s, pl.ds(node * own + r, 1), :
            ]
    backward(index_ref, pair_ref, lhs, update)
    for p in range(patches):
        total = update[p * 8 : p * 8 + slices, :] + update[p * 8 + slices : p * 8 + 2 * slices, :]
        image_ref[lo : lo + slices, p * width : (p + 1) * width] = (
            prior_ref[:, p * width : (p + 1) * width] + col_ref[p : p + 1, :] * total
        )


def exchange(value, distance, nodes):
    return lax.ppermute(value, "node", [(i, i ^ distance) for i in range(nodes)])


def body(blocks, block_row, block_patch, block_count, row_map, sinogram, start):
    nodes = lax.axis_size("node")
    count_blocks, width, _ = blocks.shape
    all_slices, pixels = start.shape
    slices = all_slices // CHAINS
    patches = pixels // width
    total_rows = row_map.shape[0]
    half = total_rows // 2
    hbm = pl.BlockSpec(memory_space=pltpu.HBM)
    smem = pl.BlockSpec(memory_space=pltpu.SMEM)
    vmem = pl.BlockSpec(memory_space=pltpu.VMEM)
    params = pltpu.CompilerParams(vmem_limit_bytes=28 * 1024 * 1024)
    small_params = pltpu.CompilerParams(vmem_limit_bytes=20 * 1024 * 1024)

    def in_hbm(value):
        return pltpu.with_memory_space_constraint(value, pltpu.HBM)

    def array(*shape):
        return jax.ShapeDtypeStruct(shape, f32)

    def sum_over_nodes(mine, other):
        value = mine + exchange(other, 1, nodes)
        distance = 2
        while distance < nodes:
            value = value + exchange(value, distance, nodes)
            distance *= 2
        return value, exchange(value, 1, nodes)

    acc_shape = pltpu.VMEM((total_rows * 8 + 8, width), f32)
    patch_shape = pltpu.VMEM((patches * 8 + 8, width), f32)

    mine, other, col, pair, index = pl.pallas_call(
        functools.partial(first_kernel, 0, slices),
        out_shape=(
            array(slices + 1, half, width),
            array(slices + 1, half, width),
            array(patches, width),
            pltpu.VMEM((count_blocks, 2 * width, width), bf16),
            pltpu.SMEM((2, count_blocks), jnp.int32),
        ),
        in_specs=[hbm] * 2 + [pl.BlockSpec(memory_space=pl.ANY)] + [hbm] * 4,
        out_specs=(vmem,) * 4 + (smem,),
        scratch_shapes=[
            pltpu.SMEM(block_row.shape, jnp.int32),
            pltpu.SMEM(block_patch.shape, jnp.int32),
            pltpu.SMEM(block_count.shape, jnp.int32),
            pltpu.SMEM(row_map.shape, jnp.int32),
            pltpu.VMEM(start.shape, f32),
            pltpu.VMEM(sinogram.shape, f32),
            pltpu.VMEM(blocks.shape, f32),
            pltpu.VMEM((patches * 16 + 16, width), f32),
            acc_shape,
            acc_shape,
            patch_shape,
            pltpu.SemaphoreType.DMA((CHUNKS,)),
            pltpu.SemaphoreType.DMA((6,)),
        ],
        compiler_params=params,
        name="first",
    )(
        in_hbm(block_row),
        in_hbm(block_patch),
        block_count,
        *map(in_hbm, (row_map, blocks, start, sinogram)),
    )

    def held():
        return (
            pltpu.with_memory_space_constraint(index, pltpu.SMEM),
            pltpu.with_memory_space_constraint(pair, pltpu.VMEM),
        )

    terms = [(mine, other)]
    for chain in range(1, CHAINS):
        terms.append(
            pl.pallas_call(
                functools.partial(second_kernel, chain * slices, slices),
                out_shape=(array(slices, half, width),) * 2,
                in_specs=[smem] + [vmem] * 3,
                out_specs=(vmem,) * 2,
                scratch_shapes=[acc_shape, patch_shape],
                compiler_params=small_params,
                name="second",
            )(*held(), start, sinogram)
        )
    images = []
    weight = None
    for chain in range(CHAINS):
        given = (weight,) if chain else ()
        got = pl.pallas_call(
            functools.partial(middle_kernel, chain * slices, slices),
            out_shape=(
                array(slices, half, width),
                array(slices, half, width),
                array(slices, pixels),
            )
            + (() if chain else (array(total_rows, width),)),
            in_specs=[smem] + [vmem] * (6 + len(given)),
            out_specs=(vmem,) * (3 if chain else 4),
            scratch_shapes=[acc_shape, patch_shape, acc_shape, patch_shape],
            compiler_params=small_params,
            name="middle",
        )(*held(), *sum_over_nodes(*terms[chain]), col, start, sinogram, *given)
        terms[chain] = got[:2]
        images.append(got[2])
        if not chain:
            weight = got[3]
    results = ()
    for chain in range(CHAINS):
        upto = (chain + 1) * slices
        results = pl.pallas_call(
            functools.partial(last_kernel, chain * slices, slices),
            out_shape=(array(upto, pixels), array(upto, sinogram.shape[1])),
            in_specs=[smem] + [vmem] * (6 + len(results)),
            out_specs=(vmem,) * 2,
            scratch_shapes=[
                acc_shape,
                pltpu.VMEM((slices, total_rows, width), f32),
                patch_shape,
            ],
            compiler_params=small_params,
            name="last",
        )(*held(), *sum_over_nodes(*terms[chain]), col, images[chain], weight, *results)
    return results


def solution(mesh):
    placed = (
        P(("grp", "node"), None, None),
        P(("grp", "node")),
        P(("grp", "node")),
        P(("grp", "node")),
        P("grp"),
        P("grp", "node"),
        P("grp", "node"),
    )
    return jax.shard_map(
        body,
        mesh=mesh,
        in_specs=placed,
        out_specs=(P("grp", "node"), P("grp", "node")),
        check_vma=False,
    )
```

```python
import functools

import jax
import jax.numpy as jnp
from jax import lax
from jax.experimental import pallas as pl
from jax.experimental.pallas import tpu as pltpu
from jax.sharding import PartitionSpec as P

CHUNKS = 4
CHAINS = 1

relax_factor = 1.9

f32 = jnp.float32
bf16 = jnp.bfloat16


def split(value):
    high = value.astype(bf16).astype(f32)
    return high, value - high


def forward_term(lhs, pair):
    both = lax.dot_general(
        lhs.astype(bf16), pair, (((1,), (1,)), ((), ())), preferred_element_type=f32
    )
    width = both.shape[1] // 2
    return both[:, :width] + both[:, width:]


def backward_term(lhs, pair):
    lhs = lhs.astype(bf16)
    return jnp.dot(
        jnp.concatenate([lhs, lhs], axis=1), pair, preferred_element_type=f32
    )


def at8(index):
    return pl.ds(pl.multiple_of(index * 8, 8), 8)


def minus_measured(acc, sino_ref, lo, slices, width, node):
    own = sino_ref.shape[1] // width
    for r in range(own):
        acc[pl.ds((node * own + r) * 8, slices), :] = -sino_ref[
            lo : lo + slices, r * width : (r + 1) * width
        ]


def write_halves(acc, slices, core, half, mine_ref, other_ref):
    for ref, side in ((mine_ref, core), (other_ref, 1 - core)):
        base = side * half * 8
        for s in range(slices):
            ref[s] = (
                acc[pl.ds(base + s, half, stride=8), :]
                + acc[pl.ds(base + s + slices, half, stride=8), :]
            )


def fill_lhs(lhs, p, stride, value, slices):
    high, low = split(value)
    lhs[p * stride : p * stride + slices, :] = high
    lhs[p * stride + slices : p * stride + 2 * slices, :] = low


def first_kernel(
    lo,
    slices,
    rows_hbm,
    patch_hbm,
    count_hbm,
    map_hbm,
    blocks_ref,
    start_hbm,
    sino_hbm,
    mine_ref,
    other_ref,
    col_ref,
    pair_ref,
    index_ref,
    rows_ref,
    patch_ref,
    count_ref,
    map_ref,
    start_ref,
    sino_ref,
    stage,
    lhs,
    acc,
    sums,
    cols,
    sems,
    small_sems,
):
    count_blocks, width, _ = blocks_ref.shape
    total_rows = map_ref.shape[0]
    half = total_rows // 2
    patches = start_ref.shape[1] // width
    node = lax.axis_index("node")
    core = lax.rem(node, 2)
    step = count_blocks // CHUNKS

    def copy(k):
        part = pl.ds(k * step, step)
        return pltpu.make_async_copy(blocks_ref.at[part], stage.at[part], sems.at[k])

    small = [
        pltpu.make_async_copy(src, dst, small_sems.at[i])
        for i, (src, dst) in enumerate(
            (
                (start_hbm, start_ref),
                (sino_hbm, sino_ref),
                (rows_hbm, rows_ref),
                (patch_hbm, patch_ref),
                (count_hbm, count_ref),
                (map_hbm, map_ref),
            )
        )
    ]
    copy(0).start()
    for one in small:
        one.start()
    for k in range(1, CHUNKS):
        copy(k).start()
    acc[...] = jnp.zeros_like(acc)
    sums[...] = jnp.zeros_like(sums)
    cols[...] = jnp.zeros_like(cols)
    lhs[...] = jnp.zeros_like(lhs)
    for one in small:
        one.wait()
    for p in range(patches):
        fill_lhs(lhs, p, 16, start_ref[lo : lo + slices, p * width : (p + 1) * width], slices)
        lhs[p * 16 + 8 : p * 16 + 9, :] = jnp.ones((1, width), f32)
    minus_measured(acc, sino_ref, lo, slices, width, node)
    count = count_ref[0]

    for k in range(CHUNKS):
        copy(k).wait()
        slots = range(k * step, (k + 1) * step)
        places = []
        terms = []
        for j in slots:
            live = j < count
            position = jnp.where(live, map_ref[rows_ref[j]], total_rows)
            patch = jnp.where(live, patch_ref[j], patches)
            index_ref[0, j] = position
            index_ref[1, j] = patch
            places.append(at8(position))
            block = stage[j]
            high = block.astype(bf16)
            pair = jnp.concatenate([high, (block - high.astype(f32)).astype(bf16)], axis=0)
            pair_ref[j] = pair
            cols[at8(patch), :] += jnp.sum(block.reshape(width // 8, 8, width), axis=0)
            terms.append(
                forward_term(lhs[pl.ds(pl.multiple_of(patch * 16, 16), 16), :], pair)
            )
        for place, term in zip(places, terms):
            acc[place, :] += term[:8]
            sums[place, :] += term[8:]

    write_halves(acc, slices, core, half, mine_ref, other_ref)
    for ref, side in ((mine_ref, core), (other_ref, 1 - core)):
        ref[slices] = sums[pl.ds(side * half * 8, half, stride=8), :]
    for p in range(patches):
        total = jnp.sum(cols[p * 8 : (p + 1) * 8, :], axis=0, keepdims=True)
        col_ref[p : p + 1, :] = relax_factor / (total + 1.0)


def weigh(slices, mine_ref, other_ref, weight_of, lhs, full, core, half):
    for ref, side in ((mine_ref, core), (other_ref, 1 - core)):
        weight = weight_of(ref, side)
        for s in range(slices):
            value = -weight * ref[s]
            high, low = split(value)
            lhs[pl.ds(side * half * 8 + s, half, stride=8), :] = high
            lhs[pl.ds(side * half * 8 + slices + s, half, stride=8), :] = low
            if full is not None:
                full[s, pl.ds(pl.multiple_of(side * half, 8), half), :] = value


def backward(index_ref, pair_ref, lhs, update):
    update[...] = jnp.zeros_like(update)
    terms = []
    for j in range(pair_ref.shape[0]):
        terms.append(backward_term(lhs[at8(index_ref[0, j]), :], pair_ref[j]))
    for j, term in enumerate(terms):
        update[at8(index_ref[1, j]), :] += term


def forward(index_ref, pair_ref, lhs, acc):
    terms = []
    for j in range(pair_ref.shape[0]):
        terms.append(forward_term(lhs[at8(index_ref[1, j]), :], pair_ref[j]))
    for j, term in enumerate(terms):
        acc[at8(index_ref[0, j]), :] += term


def second_kernel(
    lo, slices, index_ref, pair_ref, start_ref, sino_ref, mine_ref, other_ref, acc, image_lhs
):
    width = pair_ref.shape[2]
    half = mine_ref.shape[1]
    patches = start_ref.shape[1] // width
    node = lax.axis_index("node")
    image_lhs[...] = jnp.zeros_like(image_lhs)
    for p in range(patches):
        fill_lhs(image_lhs, p, 8, start_ref[lo : lo + slices, p * width : (p + 1) * width], slices)
    acc[...] = jnp.zeros_like(acc)
    minus_measured(acc, sino_ref, lo, slices, width, node)
    forward(index_ref, pair_ref, image_lhs, acc)
    write_halves(acc, slices, lax.rem(node, 2), half, mine_ref, other_ref)


def middle_kernel(
    lo,
    slices,
    index_ref,
    pair_ref,
    mine_ref,
    other_ref,
    col_ref,
    start_ref,
    sino_ref,
    *rest,
):
    given, rest = (rest[:1], rest[1:]) if lo else ((), rest)
    next_mine_ref, next_other_ref, image_ref = rest[:3]
    made, rest = (rest[3:4], rest[4:]) if not lo else ((), rest[3:])
    lhs, update, acc, image_lhs = rest
    width = pair_ref.shape[2]
    half = mine_ref.shape[1]
    patches = start_ref.shape[1] // width
    node = lax.axis_index("node")
    core = lax.rem(node, 2)

    def weight_of(ref, side):
        part = pl.ds(pl.multiple_of(side * half, 8), half)
        if given:
            return given[0][part, :]
        weight = 1.0 / (ref[slices] + 1.0)
        made[0][part, :] = weight
        return weight

    if slices < 4:
        lhs[...] = jnp.zeros_like(lhs)
        image_lhs[...] = jnp.zeros_like(image_lhs)
    lhs[2 * half * 8 :, :] = jnp.zeros((8, width), f32)
    image_lhs[patches * 8 :, :] = jnp.zeros((8, width), f32)
    weigh(slices, mine_ref, other_ref, weight_of, lhs, None, core, half)
    backward(index_ref, pair_ref, lhs, update)
    for p in range(patches):
        total = update[p * 8 : p * 8 + slices, :] + update[p * 8 + slices : p * 8 + 2 * slices, :]
        value = (
            start_ref[lo : lo + slices, p * width : (p + 1) * width]
            + col_ref[p : p + 1, :] * total
        )
        image_ref[:, p * width : (p + 1) * width] = value
        fill_lhs(image_lhs, p, 8, value, slices)
    acc[...] = jnp.zeros_like(acc)
    minus_measured(acc, sino_ref, lo, slices, width, node)
    forward(index_ref, pair_ref, image_lhs, acc)
    write_halves(acc, slices, core, half, next_mine_ref, next_other_ref)


def last_kernel(
    lo,
    slices,
    index_ref,
    pair_ref,
    mine_ref,
    other_ref,
    col_ref,
    prior_ref,
    weight_ref,
    *rest,
):
    earlier, rest = (rest[:2], rest[2:]) if lo else ((), rest)
    image_ref, weighted_ref, lhs, full, update = rest
    width = pair_ref.shape[2]
    half = mine_ref.shape[1]
    patches = prior_ref.shape[1] // width
    own = weighted_ref.shape[1] // width
    node = lax.axis_index("node")
    core = lax.rem(node, 2)

    def weight_of(ref, side):
        return weight_ref[pl.ds(pl.multiple_of(side * half, 8), half), :]

    if slices < 4:
        lhs[...] = jnp.zeros_like(lhs)
    if earlier:
        image_ref[:lo, :] = earlier[0][...]
        weighted_ref[:lo, :] = earlier[1][...]
    lhs[2 * half * 8 :, :] = jnp.zeros((8, width), f32)
    weigh(slices, mine_ref, other_ref, weight_of, lhs, full, core, half)
    for s in range(slices):
        for r in range(own):
            weighted_ref[lo + s : lo + s + 1, r * width : (r + 1) * width] = full[
                s, pl.ds(node * own + r, 1), :
            ]
    backward(index_ref, pair_ref, lhs, update)
    for p in range(patches):
        total = update[p * 8 : p * 8 + slices, :] + update[p * 8 + slices : p * 8 + 2 * slices, :]
        image_ref[lo : lo + slices, p * width : (p + 1) * width] = (
            prior_ref[:, p * width : (p + 1) * width] + col_ref[p : p + 1, :] * total
        )


def exchange(value, distance, nodes):
    return lax.ppermute(value, "node", [(i, i ^ distance) for i in range(nodes)])


def body(blocks, block_row, block_patch, block_count, row_map, sinogram, start):
    nodes = lax.axis_size("node")
    count_blocks, width, _ = blocks.shape
    all_slices, pixels = start.shape
    slices = all_slices // CHAINS
    patches = pixels // width
    total_rows = row_map.shape[0]
    half = total_rows // 2
    hbm = pl.BlockSpec(memory_space=pltpu.HBM)
    smem = pl.BlockSpec(memory_space=pltpu.SMEM)
    vmem = pl.BlockSpec(memory_space=pltpu.VMEM)
    params = pltpu.CompilerParams(vmem_limit_bytes=28 * 1024 * 1024)
    small_params = pltpu.CompilerParams(vmem_limit_bytes=20 * 1024 * 1024)

    def in_hbm(value):
        return pltpu.with_memory_space_constraint(value, pltpu.HBM)

    def array(*shape):
        return jax.ShapeDtypeStruct(shape, f32)

    distances = [2**k for k in range(1, nodes.bit_length() - 1)]
    swapped = distances[1::-1] + distances[2:]

    def sum_over_nodes(mine, other):
        cut = 2
        values = [
            m + exchange(o, 1, nodes)
            for m, o in ((mine[:cut], other[:cut]), (mine[cut:], other[cut:]))
        ]
        for pair in zip(distances, swapped):
            got = [exchange(v, d, nodes) for v, d in zip(values, pair)]
            values = [v + g for v, g in zip(values, got)]
        others = [exchange(v, 1, nodes) for v in values]
        return jnp.concatenate(values), jnp.concatenate(others)

    acc_shape = pltpu.VMEM((total_rows * 8 + 8, width), f32)
    patch_shape = pltpu.VMEM((patches * 8 + 8, width), f32)

    mine, other, col, pair, index = pl.pallas_call(
        functools.partial(first_kernel, 0, slices),
        out_shape=(
            array(slices + 1, half, width),
            array(slices + 1, half, width),
            array(patches, width),
            pltpu.VMEM((count_blocks, 2 * width, width), bf16),
            pltpu.SMEM((2, count_blocks), jnp.int32),
        ),
        in_specs=[hbm] * 2 + [pl.BlockSpec(memory_space=pl.ANY)] + [hbm] * 4,
        out_specs=(vmem,) * 4 + (smem,),
        scratch_shapes=[
            pltpu.SMEM(block_row.shape, jnp.int32),
            pltpu.SMEM(block_patch.shape, jnp.int32),
            pltpu.SMEM(block_count.shape, jnp.int32),
            pltpu.SMEM(row_map.shape, jnp.int32),
            pltpu.VMEM(start.shape, f32),
            pltpu.VMEM(sinogram.shape, f32),
            pltpu.VMEM(blocks.shape, f32),
            pltpu.VMEM((patches * 16 + 16, width), f32),
            acc_shape,
            acc_shape,
            patch_shape,
            pltpu.SemaphoreType.DMA((CHUNKS,)),
            pltpu.SemaphoreType.DMA((6,)),
        ],
        compiler_params=params,
        name="first",
    )(
        in_hbm(block_row),
        in_hbm(block_patch),
        block_count,
        *map(in_hbm, (row_map, blocks, start, sinogram)),
    )

    def held():
        return (
            pltpu.with_memory_space_constraint(index, pltpu.SMEM),
            pltpu.with_memory_space_constraint(pair, pltpu.VMEM),
        )

    terms = [(mine, other)]
    for chain in range(1, CHAINS):
        terms.append(
            pl.pallas_call(
                functools.partial(second_kernel, chain * slices, slices),
                out_shape=(array(slices, half, width),) * 2,
                in_specs=[smem] + [vmem] * 3,
                out_specs=(vmem,) * 2,
                scratch_shapes=[acc_shape, patch_shape],
                compiler_params=small_params,
                name="second",
            )(*held(), start, sinogram)
        )
    images = []
    weight = None
    for chain in range(CHAINS):
        given = (weight,) if chain else ()
        got = pl.pallas_call(
            functools.partial(middle_kernel, chain * slices, slices),
            out_shape=(
                array(slices, half, width),
                array(slices, half, width),
                array(slices, pixels),
            )
            + (() if chain else (array(total_rows, width),)),
            in_specs=[smem] + [vmem] * (6 + len(given)),
            out_specs=(vmem,) * (3 if chain else 4),
            scratch_shapes=[acc_shape, patch_shape, acc_shape, patch_shape],
            compiler_params=small_params,
            name="middle",
        )(*held(), *sum_over_nodes(*terms[chain]), col, start, sinogram, *given)
        terms[chain] = got[:2]
        images.append(got[2])
        if not chain:
            weight = got[3]
    results = ()
    for chain in range(CHAINS):
        upto = (chain + 1) * slices
        results = pl.pallas_call(
            functools.partial(last_kernel, chain * slices, slices),
            out_shape=(array(upto, pixels), array(upto, sinogram.shape[1])),
            in_specs=[smem] + [vmem] * (6 + len(results)),
            out_specs=(vmem,) * 2,
            scratch_shapes=[
                acc_shape,
                pltpu.VMEM((slices, total_rows, width), f32),
                patch_shape,
            ],
            compiler_params=small_params,
            name="last",
        )(*held(), *sum_over_nodes(*terms[chain]), col, images[chain], weight, *results)
    return results


def solution(mesh):
    placed = (
        P(("grp", "node"), None, None),
        P(("grp", "node")),
        P(("grp", "node")),
        P(("grp", "node")),
        P("grp"),
        P("grp", "node"),
        P("grp", "node"),
    )
    return jax.shard_map(
        body,
        mesh=mesh,
        in_specs=placed,
        out_specs=(P("grp", "node"), P("grp", "node")),
        check_vma=False,
    )
```

```python
import functools

import jax
import jax.numpy as jnp
from jax import lax
from jax.experimental import pallas as pl
from jax.experimental.pallas import tpu as pltpu
from jax.sharding import PartitionSpec as P

CHUNKS = 4
WAYS = 4
CHAINS = 1

relax_factor = 1.9

f32 = jnp.float32
bf16 = jnp.bfloat16


def split(value):
    high = value.astype(bf16).astype(f32)
    return high, value - high


def product(lhs, pair):
    lhs = lhs.astype(bf16)
    return jnp.dot(
        jnp.concatenate([lhs, lhs], axis=1), pair, preferred_element_type=f32
    )


def at8(index):
    return pl.ds(pl.multiple_of(index * 8, 8), 8)


def minus_measured(acc, sino_ref, lo, slices, width, node):
    own = sino_ref.shape[1] // width
    for r in range(own):
        acc[pl.ds((node * own + r) * 8, slices), :] = -sino_ref[
            lo : lo + slices, r * width : (r + 1) * width
        ]


def write_halves(acc, slices, core, half, mine_ref, other_ref):
    for ref, side in ((mine_ref, core), (other_ref, 1 - core)):
        base = side * half * 8
        for s in range(slices):
            ref[s] = (
                acc[pl.ds(base + s, half, stride=8), :]
                + acc[pl.ds(base + s + slices, half, stride=8), :]
            )


def fill_lhs(lhs, p, stride, value, slices):
    high, low = split(value)
    lhs[p * stride : p * stride + slices, :] = high
    lhs[p * stride + slices : p * stride + 2 * slices, :] = low


def first_kernel(
    lo,
    slices,
    rows_hbm,
    patch_hbm,
    count_hbm,
    map_hbm,
    blocks_ref,
    start_hbm,
    sino_hbm,
    mine_ref,
    other_ref,
    col_ref,
    pair_ref,
    turned_ref,
    index_ref,
    rows_ref,
    patch_ref,
    count_ref,
    map_ref,
    start_ref,
    sino_ref,
    stage,
    lhs,
    acc,
    sums,
    sems,
    small_sems,
    *cols,
):
    count_blocks, width, _ = blocks_ref.shape
    total_rows = map_ref.shape[0]
    half = total_rows // 2
    patches = start_ref.shape[1] // width
    node = lax.axis_index("node")
    core = lax.rem(node, 2)
    step = count_blocks // CHUNKS

    def copy(k):
        part = pl.ds(k * step, step)
        return pltpu.make_async_copy(blocks_ref.at[part], stage.at[part], sems.at[k])

    small = [
        pltpu.make_async_copy(src, dst, small_sems.at[i])
        for i, (src, dst) in enumerate(
            (
                (start_hbm, start_ref),
                (sino_hbm, sino_ref),
                (rows_hbm, rows_ref),
                (patch_hbm, patch_ref),
                (count_hbm, count_ref),
                (map_hbm, map_ref),
            )
        )
    ]
    copy(0).start()
    for one in small:
        one.start()
    for k in range(1, CHUNKS):
        copy(k).start()
    acc[...] = jnp.zeros_like(acc)
    sums[...] = jnp.zeros_like(sums)
    for one in cols:
        one[...] = jnp.zeros_like(one)
    lhs[...] = jnp.zeros_like(lhs)
    for one in small:
        one.wait()
    for p in range(patches):
        fill_lhs(lhs, p, 16, start_ref[lo : lo + slices, p * width : (p + 1) * width], slices)
        lhs[p * 16 + 8 : p * 16 + 9, :] = jnp.ones((1, width), f32)
    minus_measured(acc, sino_ref, lo, slices, width, node)
    count = count_ref[0]

    for k in range(CHUNKS):
        copy(k).wait()
        slots = range(k * step, (k + 1) * step)
        places = []
        terms = []
        for j in slots:
            live = j < count
            position = jnp.where(live, map_ref[rows_ref[j]], total_rows)
            patch = jnp.where(live, patch_ref[j], patches)
            index_ref[0, j] = position
            index_ref[1, j] = patch
            places.append(at8(position))
            block = stage[j]
            high = block.astype(bf16)
            low = block - high.astype(f32)
            pair_ref[j, :width, :] = high
            pair_ref[j, width:, :] = low.astype(bf16)
            other = block.T
            high = other.astype(bf16)
            turned = jnp.concatenate([high, (other - high.astype(f32)).astype(bf16)], axis=0)
            turned_ref[j] = turned
            cols[j % WAYS][at8(patch), :] += jnp.sum(block.reshape(width // 8, 8, width), axis=0)
            terms.append(
                product(lhs[pl.ds(pl.multiple_of(patch * 16, 16), 16), :], turned)
            )
        for place, term in zip(places, terms):
            acc[place, :] += term[:8]
            sums[place, :] += term[8:]

    write_halves(acc, slices, core, half, mine_ref, other_ref)
    for ref, side in ((mine_ref, core), (other_ref, 1 - core)):
        ref[slices] = sums[pl.ds(side * half * 8, half, stride=8), :]
    for p in range(patches):
        total = cols[0][at8(p), :]
        for one in cols[1:]:
            total = total + one[at8(p), :]
        total = jnp.sum(total, axis=0, keepdims=True)
        col_ref[p : p + 1, :] = relax_factor / (total + 1.0)


def weigh(slices, mine_ref, other_ref, weight_of, lhs, full, core, half):
    for ref, side in ((mine_ref, core), (other_ref, 1 - core)):
        weight = weight_of(ref, side)
        for s in range(slices):
            value = -weight * ref[s]
            high, low = split(value)
            lhs[pl.ds(side * half * 8 + s, half, stride=8), :] = high
            lhs[pl.ds(side * half * 8 + slices + s, half, stride=8), :] = low
            if full is not None:
                full[s, pl.ds(pl.multiple_of(side * half, 8), half), :] = value


def patch_total(update, p, slices):
    total = update[0][at8(p), :]
    for one in update[1:]:
        total = total + one[at8(p), :]
    return total[:slices] + total[slices : 2 * slices]


def backward(index_ref, pair_ref, lhs, update):
    for one in update:
        one[...] = jnp.zeros_like(one)
    terms = []
    for j in range(pair_ref.shape[0]):
        terms.append(product(lhs[at8(index_ref[0, j]), :], pair_ref[j]))
    for j, term in enumerate(terms):
        update[j % WAYS][at8(index_ref[1, j]), :] += term


def forward(index_ref, turned_ref, lhs, acc):
    terms = []
    for j in range(turned_ref.shape[0]):
        terms.append(product(lhs[at8(index_ref[1, j]), :], turned_ref[j]))
    for j, term in enumerate(terms):
        acc[at8(index_ref[0, j]), :] += term


def middle_kernel(
    lo,
    slices,
    index_ref,
    pair_ref,
    turned_ref,
    mine_ref,
    other_ref,
    col_ref,
    start_ref,
    sino_ref,
    *rest,
):
    given, rest = (rest[:1], rest[1:]) if lo else ((), rest)
    next_mine_ref, next_other_ref, image_ref = rest[:3]
    made, rest = (rest[3:4], rest[4:]) if not lo else ((), rest[3:])
    lhs, acc, image_lhs = rest[:3]
    update = rest[3:]
    width = pair_ref.shape[2]
    half = mine_ref.shape[1]
    patches = start_ref.shape[1] // width
    node = lax.axis_index("node")
    core = lax.rem(node, 2)

    def weight_of(ref, side):
        part = pl.ds(pl.multiple_of(side * half, 8), half)
        if given:
            return given[0][part, :]
        weight = 1.0 / (ref[slices] + 1.0)
        made[0][part, :] = weight
        return weight

    if slices < 4:
        lhs[...] = jnp.zeros_like(lhs)
        image_lhs[...] = jnp.zeros_like(image_lhs)
    lhs[2 * half * 8 :, :] = jnp.zeros((8, width), f32)
    image_lhs[patches * 8 :, :] = jnp.zeros((8, width), f32)
    weigh(slices, mine_ref, other_ref, weight_of, lhs, None, core, half)
    backward(index_ref, pair_ref, lhs, update)
    for p in range(patches):
        total = patch_total(update, p, slices)
        value = (
            start_ref[lo : lo + slices, p * width : (p + 1) * width]
            + col_ref[p : p + 1, :] * total
        )
        image_ref[:, p * width : (p + 1) * width] = value
        fill_lhs(image_lhs, p, 8, value, slices)
    acc[...] = jnp.zeros_like(acc)
    minus_measured(acc, sino_ref, lo, slices, width, node)
    forward(index_ref, turned_ref, image_lhs, acc)
    write_halves(acc, slices, core, half, next_mine_ref, next_other_ref)


def last_kernel(
    lo,
    slices,
    index_ref,
    pair_ref,
    mine_ref,
    other_ref,
    col_ref,
    prior_ref,
    weight_ref,
    *rest,
):
    earlier, rest = (rest[:2], rest[2:]) if lo else ((), rest)
    image_ref, weighted_ref, lhs, full = rest[:4]
    update = rest[4:]
    width = pair_ref.shape[2]
    half = mine_ref.shape[1]
    patches = prior_ref.shape[1] // width
    own = weighted_ref.shape[1] // width
    node = lax.axis_index("node")
    core = lax.rem(node, 2)

    def weight_of(ref, side):
        return weight_ref[pl.ds(pl.multiple_of(side * half, 8), half), :]

    if slices < 4:
        lhs[...] = jnp.zeros_like(lhs)
    if earlier:
        image_ref[:lo, :] = earlier[0][...]
        weighted_ref[:lo, :] = earlier[1][...]
    lhs[2 * half * 8 :, :] = jnp.zeros((8, width), f32)
    weigh(slices, mine_ref, other_ref, weight_of, lhs, full, core, half)
    for s in range(slices):
        for r in range(own):
            weighted_ref[lo + s : lo + s + 1, r * width : (r + 1) * width] = full[
                s, pl.ds(node * own + r, 1), :
            ]
    backward(index_ref, pair_ref, lhs, update)
    for p in range(patches):
        total = patch_total(update, p, slices)
        image_ref[lo : lo + slices, p * width : (p + 1) * width] = (
            prior_ref[:, p * width : (p + 1) * width] + col_ref[p : p + 1, :] * total
        )


def exchange(value, distance, nodes):
    return lax.ppermute(value, "node", [(i, i ^ distance) for i in range(nodes)])


def body(blocks, block_row, block_patch, block_count, row_map, sinogram, start):
    nodes = lax.axis_size("node")
    count_blocks, width, _ = blocks.shape
    all_slices, pixels = start.shape
    slices = all_slices // CHAINS
    patches = pixels // width
    total_rows = row_map.shape[0]
    half = total_rows // 2
    hbm = pl.BlockSpec(memory_space=pltpu.HBM)
    smem = pl.BlockSpec(memory_space=pltpu.SMEM)
    vmem = pl.BlockSpec(memory_space=pltpu.VMEM)
    params = pltpu.CompilerParams(vmem_limit_bytes=28 * 1024 * 1024)
    small_params = pltpu.CompilerParams(vmem_limit_bytes=20 * 1024 * 1024)

    def in_hbm(value):
        return pltpu.with_memory_space_constraint(value, pltpu.HBM)

    def array(*shape):
        return jax.ShapeDtypeStruct(shape, f32)

    distances = [2**k for k in range(1, nodes.bit_length() - 1)]
    swapped = distances[1::-1] + distances[2:]

    def sum_over_nodes(mine, other):
        cut = 2
        values = [
            m + exchange(o, 1, nodes)
            for m, o in ((mine[:cut], other[:cut]), (mine[cut:], other[cut:]))
        ]
        for pair in zip(distances, swapped):
            got = [exchange(v, d, nodes) for v, d in zip(values, pair)]
            values = [v + g for v, g in zip(values, got)]
        others = [exchange(v, 1, nodes) for v in values]
        return jnp.concatenate(values), jnp.concatenate(others)

    acc_shape = pltpu.VMEM((total_rows * 8 + 8, width), f32)
    patch_shape = pltpu.VMEM((patches * 8 + 8, width), f32)

    mine, other, col, pair, turned, index = pl.pallas_call(
        functools.partial(first_kernel, 0, slices),
        out_shape=(
            array(slices + 1, half, width),
            array(slices + 1, half, width),
            array(patches, width),
            pltpu.VMEM((count_blocks, 2 * width, width), bf16),
            pltpu.VMEM((count_blocks, 2 * width, width), bf16),
            pltpu.SMEM((2, count_blocks), jnp.int32),
        ),
        in_specs=[hbm] * 2 + [pl.BlockSpec(memory_space=pl.ANY)] + [hbm] * 4,
        out_specs=(vmem,) * 5 + (smem,),
        scratch_shapes=[
            pltpu.SMEM(block_row.shape, jnp.int32),
            pltpu.SMEM(block_patch.shape, jnp.int32),
            pltpu.SMEM(block_count.shape, jnp.int32),
            pltpu.SMEM(row_map.shape, jnp.int32),
            pltpu.VMEM(start.shape, f32),
            pltpu.VMEM(sinogram.shape, f32),
            pltpu.VMEM(blocks.shape, f32),
            pltpu.VMEM((patches * 16 + 16, width), f32),
            acc_shape,
            acc_shape,
            pltpu.SemaphoreType.DMA((CHUNKS,)),
            pltpu.SemaphoreType.DMA((6,)),
        ]
        + [patch_shape] * WAYS,
        compiler_params=params,
        name="first",
    )(
        in_hbm(block_row),
        in_hbm(block_patch),
        block_count,
        *map(in_hbm, (row_map, blocks, start, sinogram)),
    )

    def held():
        return (
            pltpu.with_memory_space_constraint(index, pltpu.SMEM),
            pltpu.with_memory_space_constraint(pair, pltpu.VMEM),
        )

    terms = [(mine, other)]
    images = []
    weight = None
    for chain in range(CHAINS):
        given = (weight,) if chain else ()
        got = pl.pallas_call(
            functools.partial(middle_kernel, chain * slices, slices),
            out_shape=(
                array(slices, half, width),
                array(slices, half, width),
                array(slices, pixels),
            )
            + (() if chain else (array(total_rows, width),)),
            in_specs=[smem] + [vmem] * (7 + len(given)),
            out_specs=(vmem,) * (3 if chain else 4),
            scratch_shapes=[acc_shape, acc_shape, patch_shape] + [patch_shape] * WAYS,
            compiler_params=small_params,
            name="middle",
        )(
            *held(),
            pltpu.with_memory_space_constraint(turned, pltpu.VMEM),
            *sum_over_nodes(*terms[chain]),
            col, start, sinogram, *given)
        terms[chain] = got[:2]
        images.append(got[2])
        if not chain:
            weight = got[3]
    results = ()
    for chain in range(CHAINS):
        upto = (chain + 1) * slices
        results = pl.pallas_call(
            functools.partial(last_kernel, chain * slices, slices),
            out_shape=(array(upto, pixels), array(upto, sinogram.shape[1])),
            in_specs=[smem] + [vmem] * (6 + len(results)),
            out_specs=(vmem,) * 2,
            scratch_shapes=[
                acc_shape,
                pltpu.VMEM((slices, total_rows, width), f32),
            ]
            + [patch_shape] * WAYS,
            compiler_params=small_params,
            name="last",
        )(*held(), *sum_over_nodes(*terms[chain]), col, images[chain], weight, *results)
    return results


def solution(mesh):
    placed = (
        P(("grp", "node"), None, None),
        P(("grp", "node")),
        P(("grp", "node")),
        P(("grp", "node")),
        P("grp"),
        P("grp", "node"),
        P("grp", "node"),
    )
    return jax.shard_map(
        body,
        mesh=mesh,
        in_specs=placed,
        out_specs=(P("grp", "node"), P("grp", "node")),
        check_vma=False,
    )
```

```python
import functools

import jax
import jax.numpy as jnp
from jax import lax
from jax.experimental import pallas as pl
from jax.experimental.pallas import tpu as pltpu
from jax.sharding import PartitionSpec as P

CHUNKS = 3
WAYS = 4
CHAINS = 1

relax_factor = 1.9

f32 = jnp.float32
bf16 = jnp.bfloat16


def split(value):
    high = value.astype(bf16).astype(f32)
    return high, value - high


def product(lhs, pair):
    lhs = lhs.astype(bf16)
    return jnp.dot(
        jnp.concatenate([lhs, lhs], axis=1), pair, preferred_element_type=f32
    )


def at8(index):
    return pl.ds(pl.multiple_of(index * 8, 8), 8)


def minus_measured(acc, sino_ref, lo, slices, width, node):
    own = sino_ref.shape[1] // width
    for r in range(own):
        acc[pl.ds((node * own + r) * 8, slices), :] = -sino_ref[
            lo : lo + slices, r * width : (r + 1) * width
        ]


def write_halves(acc, slices, core, half, mine_ref, other_ref):
    for ref, side in ((mine_ref, core), (other_ref, 1 - core)):
        base = side * half * 8
        for s in range(slices):
            ref[s] = (
                acc[pl.ds(base + s, half, stride=8), :]
                + acc[pl.ds(base + s + slices, half, stride=8), :]
            )


def fill_lhs(lhs, p, stride, value, slices):
    high, low = split(value)
    lhs[p * stride : p * stride + slices, :] = high
    lhs[p * stride + slices : p * stride + 2 * slices, :] = low


def first_kernel(
    lo,
    slices,
    rows_hbm,
    patch_hbm,
    count_hbm,
    map_hbm,
    blocks_ref,
    start_hbm,
    sino_hbm,
    mine_ref,
    other_ref,
    stage,
    turned_ref,
    index_ref,
    rows_ref,
    patch_ref,
    count_ref,
    map_ref,
    start_ref,
    sino_ref,
    lhs,
    acc,
    sums,
    sems,
    small_sems,
):
    count_blocks, width, _ = blocks_ref.shape
    total_rows = map_ref.shape[0]
    half = total_rows // 2
    patches = start_ref.shape[1] // width
    node = lax.axis_index("node")
    core = lax.rem(node, 2)
    step = count_blocks // CHUNKS

    def copy(k):
        part = pl.ds(k * step, step)
        return pltpu.make_async_copy(blocks_ref.at[part], stage.at[part], sems.at[k])

    small = [
        pltpu.make_async_copy(src, dst, small_sems.at[i])
        for i, (src, dst) in enumerate(
            (
                (start_hbm, start_ref),
                (sino_hbm, sino_ref),
                (rows_hbm, rows_ref),
                (patch_hbm, patch_ref),
                (count_hbm, count_ref),
                (map_hbm, map_ref),
            )
        )
    ]
    copy(0).start()
    for one in small:
        one.start()
    for k in range(1, CHUNKS):
        copy(k).start()
    acc[...] = jnp.zeros_like(acc)
    sums[...] = jnp.zeros_like(sums)
    lhs[...] = jnp.zeros_like(lhs)
    for one in small:
        one.wait()
    for p in range(patches):
        fill_lhs(lhs, p, 16, start_ref[lo : lo + slices, p * width : (p + 1) * width], slices)
        lhs[p * 16 + 8 : p * 16 + 9, :] = jnp.ones((1, width), f32)
    minus_measured(acc, sino_ref, lo, slices, width, node)
    count = count_ref[0]

    for k in range(CHUNKS):
        copy(k).wait()
        slots = range(k * step, (k + 1) * step)
        places = []
        terms = []
        for j in slots:
            live = j < count
            position = jnp.where(live, map_ref[rows_ref[j]], total_rows)
            patch = jnp.where(live, patch_ref[j], patches)
            index_ref[0, j] = position
            index_ref[1, j] = patch
            places.append(at8(position))
            block = stage[j].T
            high = block.astype(bf16)
            turned = jnp.concatenate([high, (block - high.astype(f32)).astype(bf16)], axis=0)
            turned_ref[j] = turned
            terms.append(
                product(lhs[pl.ds(pl.multiple_of(patch * 16, 16), 16), :], turned)
            )
        for place, term in zip(places, terms):
            acc[place, :] += term[:8]
            sums[place, :] += term[8:]

    write_halves(acc, slices, core, half, mine_ref, other_ref)
    for ref, side in ((mine_ref, core), (other_ref, 1 - core)):
        ref[slices] = sums[pl.ds(side * half * 8, half, stride=8), :]


def prepare_kernel(index_ref, stage, col_ref, pair_ref, *cols):
    count_blocks, width, _ = stage.shape
    patches = col_ref.shape[0]
    for one in cols:
        one[...] = jnp.zeros_like(one)
    for j in range(count_blocks):
        block = stage[j]
        high = block.astype(bf16)
        pair_ref[j, :width, :] = high
        pair_ref[j, width:, :] = (block - high.astype(f32)).astype(bf16)
        cols[j % WAYS][at8(index_ref[1, j]), :] += jnp.sum(
            block.reshape(width // 8, 8, width), axis=0
        )
    for p in range(patches):
        total = cols[0][at8(p), :]
        for one in cols[1:]:
            total = total + one[at8(p), :]
        total = jnp.sum(total, axis=0, keepdims=True)
        col_ref[p : p + 1, :] = relax_factor / (total + 1.0)


def weigh(slices, mine_ref, other_ref, weight_of, lhs, full, core, half):
    for ref, side in ((mine_ref, core), (other_ref, 1 - core)):
        weight = weight_of(ref, side)
        for s in range(slices):
            value = -weight * ref[s]
            high, low = split(value)
            lhs[pl.ds(side * half * 8 + s, half, stride=8), :] = high
            lhs[pl.ds(side * half * 8 + slices + s, half, stride=8), :] = low
            if full is not None:
                full[s, pl.ds(pl.multiple_of(side * half, 8), half), :] = value


def patch_total(update, p, slices):
    total = update[0][at8(p), :]
    for one in update[1:]:
        total = total + one[at8(p), :]
    return total[:slices] + total[slices : 2 * slices]


def backward(index_ref, pair_ref, lhs, update):
    for one in update:
        one[...] = jnp.zeros_like(one)
    terms = []
    for j in range(pair_ref.shape[0]):
        terms.append(product(lhs[at8(index_ref[0, j]), :], pair_ref[j]))
    for j, term in enumerate(terms):
        update[j % WAYS][at8(index_ref[1, j]), :] += term


def forward(index_ref, turned_ref, lhs, acc):
    terms = []
    for j in range(turned_ref.shape[0]):
        terms.append(product(lhs[at8(index_ref[1, j]), :], turned_ref[j]))
    for j, term in enumerate(terms):
        acc[at8(index_ref[0, j]), :] += term


def middle_kernel(
    lo,
    slices,
    index_ref,
    pair_ref,
    turned_ref,
    mine_ref,
    other_ref,
    col_ref,
    start_ref,
    sino_ref,
    *rest,
):
    given, rest = (rest[:1], rest[1:]) if lo else ((), rest)
    next_mine_ref, next_other_ref, image_ref = rest[:3]
    made, rest = (rest[3:4], rest[4:]) if not lo else ((), rest[3:])
    lhs, acc, image_lhs = rest[:3]
    update = rest[3:]
    width = pair_ref.shape[2]
    half = mine_ref.shape[1]
    patches = start_ref.shape[1] // width
    node = lax.axis_index("node")
    core = lax.rem(node, 2)

    def weight_of(ref, side):
        part = pl.ds(pl.multiple_of(side * half, 8), half)
        if given:
            return given[0][part, :]
        weight = 1.0 / (ref[slices] + 1.0)
        made[0][part, :] = weight
        return weight

    if slices < 4:
        lhs[...] = jnp.zeros_like(lhs)
        image_lhs[...] = jnp.zeros_like(image_lhs)
    lhs[2 * half * 8 :, :] = jnp.zeros((8, width), f32)
    image_lhs[patches * 8 :, :] = jnp.zeros((8, width), f32)
    weigh(slices, mine_ref, other_ref, weight_of, lhs, None, core, half)
    backward(index_ref, pair_ref, lhs, update)
    for p in range(patches):
        total = patch_total(update, p, slices)
        value = (
            start_ref[lo : lo + slices, p * width : (p + 1) * width]
            + col_ref[p : p + 1, :] * total
        )
        image_ref[:, p * width : (p + 1) * width] = value
        fill_lhs(image_lhs, p, 8, value, slices)
    acc[...] = jnp.zeros_like(acc)
    minus_measured(acc, sino_ref, lo, slices, width, node)
    forward(index_ref, turned_ref, image_lhs, acc)
    write_halves(acc, slices, core, half, next_mine_ref, next_other_ref)


def last_kernel(
    lo,
    slices,
    index_ref,
    pair_ref,
    mine_ref,
    other_ref,
    col_ref,
    prior_ref,
    weight_ref,
    *rest,
):
    earlier, rest = (rest[:2], rest[2:]) if lo else ((), rest)
    image_ref, weighted_ref, lhs, full = rest[:4]
    update = rest[4:]
    width = pair_ref.shape[2]
    half = mine_ref.shape[1]
    patches = prior_ref.shape[1] // width
    own = weighted_ref.shape[1] // width
    node = lax.axis_index("node")
    core = lax.rem(node, 2)

    def weight_of(ref, side):
        return weight_ref[pl.ds(pl.multiple_of(side * half, 8), half), :]

    if slices < 4:
        lhs[...] = jnp.zeros_like(lhs)
    if earlier:
        image_ref[:lo, :] = earlier[0][...]
        weighted_ref[:lo, :] = earlier[1][...]
    lhs[2 * half * 8 :, :] = jnp.zeros((8, width), f32)
    weigh(slices, mine_ref, other_ref, weight_of, lhs, full, core, half)
    for s in range(slices):
        for r in range(own):
            weighted_ref[lo + s : lo + s + 1, r * width : (r + 1) * width] = full[
                s, pl.ds(node * own + r, 1), :
            ]
    backward(index_ref, pair_ref, lhs, update)
    for p in range(patches):
        total = patch_total(update, p, slices)
        image_ref[lo : lo + slices, p * width : (p + 1) * width] = (
            prior_ref[:, p * width : (p + 1) * width] + col_ref[p : p + 1, :] * total
        )


def exchange(value, distance, nodes):
    return lax.ppermute(value, "node", [(i, i ^ distance) for i in range(nodes)])


def body(blocks, block_row, block_patch, block_count, row_map, sinogram, start):
    nodes = lax.axis_size("node")
    count_blocks, width, _ = blocks.shape
    all_slices, pixels = start.shape
    slices = all_slices // CHAINS
    patches = pixels // width
    total_rows = row_map.shape[0]
    half = total_rows // 2
    hbm = pl.BlockSpec(memory_space=pltpu.HBM)
    smem = pl.BlockSpec(memory_space=pltpu.SMEM)
    vmem = pl.BlockSpec(memory_space=pltpu.VMEM)
    params = pltpu.CompilerParams(vmem_limit_bytes=28 * 1024 * 1024)
    small_params = pltpu.CompilerParams(vmem_limit_bytes=20 * 1024 * 1024)

    def in_hbm(value):
        return pltpu.with_memory_space_constraint(value, pltpu.HBM)

    def array(*shape):
        return jax.ShapeDtypeStruct(shape, f32)

    distances = [2**k for k in range(1, nodes.bit_length() - 1)]
    swapped = distances[1::-1] + distances[2:]

    def sum_over_nodes(mine, other):
        cut = mine.shape[0] - 2
        values = [
            m + exchange(o, 1, nodes)
            for m, o in ((mine[:cut], other[:cut]), (mine[cut:], other[cut:]))
        ]
        for pair in zip(distances, swapped):
            got = [exchange(v, d, nodes) for v, d in zip(values, pair)]
            values = [v + g for v, g in zip(values, got)]
        others = [exchange(v, 1, nodes) for v in values]
        return jnp.concatenate(values), jnp.concatenate(others)

    acc_shape = pltpu.VMEM((total_rows * 8 + 8, width), f32)
    patch_shape = pltpu.VMEM((patches * 8 + 8, width), f32)

    mine, other, stage, turned, index = pl.pallas_call(
        functools.partial(first_kernel, 0, slices),
        out_shape=(
            array(slices + 1, half, width),
            array(slices + 1, half, width),
            pltpu.VMEM(blocks.shape, f32),
            pltpu.VMEM((count_blocks, 2 * width, width), bf16),
            pltpu.SMEM((2, count_blocks), jnp.int32),
        ),
        in_specs=[hbm] * 2 + [pl.BlockSpec(memory_space=pl.ANY)] + [hbm] * 4,
        out_specs=(vmem,) * 4 + (smem,),
        scratch_shapes=[
            pltpu.SMEM(block_row.shape, jnp.int32),
            pltpu.SMEM(block_patch.shape, jnp.int32),
            pltpu.SMEM(block_count.shape, jnp.int32),
            pltpu.SMEM(row_map.shape, jnp.int32),
            pltpu.VMEM(start.shape, f32),
            pltpu.VMEM(sinogram.shape, f32),
            pltpu.VMEM((patches * 16 + 16, width), f32),
            acc_shape,
            acc_shape,
            pltpu.SemaphoreType.DMA((CHUNKS,)),
            pltpu.SemaphoreType.DMA((6,)),
        ],
        compiler_params=params,
        name="first",
    )(
        in_hbm(block_row),
        in_hbm(block_patch),
        block_count,
        *map(in_hbm, (row_map, blocks, start, sinogram)),
    )

    col, pair = pl.pallas_call(
        prepare_kernel,
        out_shape=(
            array(patches, width),
            pltpu.VMEM((count_blocks, 2 * width, width), bf16),
        ),
        in_specs=[smem, vmem],
        out_specs=(vmem,) * 2,
        scratch_shapes=[patch_shape] * WAYS,
        compiler_params=pltpu.CompilerParams(vmem_limit_bytes=8 * 1024 * 1024),
        cost_estimate=pl.CostEstimate(
            flops=0, bytes_accessed=2 * blocks.size * 4, transcendentals=0
        ),
        name="prepare",
    )(
        pltpu.with_memory_space_constraint(index, pltpu.SMEM),
        pltpu.with_memory_space_constraint(stage, pltpu.VMEM),
    )

    def held():
        return (
            pltpu.with_memory_space_constraint(index, pltpu.SMEM),
            pltpu.with_memory_space_constraint(pair, pltpu.VMEM),
        )

    terms = [(mine, other)]
    images = []
    weight = None
    for chain in range(CHAINS):
        given = (weight,) if chain else ()
        got = pl.pallas_call(
            functools.partial(middle_kernel, chain * slices, slices),
            out_shape=(
                array(slices, half, width),
                array(slices, half, width),
                array(slices, pixels),
            )
            + (() if chain else (array(total_rows, width),)),
            in_specs=[smem] + [vmem] * (7 + len(given)),
            out_specs=(vmem,) * (3 if chain else 4),
            scratch_shapes=[acc_shape, acc_shape, patch_shape] + [patch_shape] * WAYS,
            compiler_params=small_params,
            name="middle",
        )(
            *held(),
            pltpu.with_memory_space_constraint(turned, pltpu.VMEM),
            *sum_over_nodes(*terms[chain]),
            col, start, sinogram, *given)
        terms[chain] = got[:2]
        images.append(got[2])
        if not chain:
            weight = got[3]
    results = ()
    for chain in range(CHAINS):
        upto = (chain + 1) * slices
        results = pl.pallas_call(
            functools.partial(last_kernel, chain * slices, slices),
            out_shape=(array(upto, pixels), array(upto, sinogram.shape[1])),
            in_specs=[smem] + [vmem] * (6 + len(results)),
            out_specs=(vmem,) * 2,
            scratch_shapes=[
                acc_shape,
                pltpu.VMEM((slices, total_rows, width), f32),
            ]
            + [patch_shape] * WAYS,
            compiler_params=small_params,
            name="last",
        )(*held(), *sum_over_nodes(*terms[chain]), col, images[chain], weight, *results)
    return results


def solution(mesh):
    placed = (
        P(("grp", "node"), None, None),
        P(("grp", "node")),
        P(("grp", "node")),
        P(("grp", "node")),
        P("grp"),
        P("grp", "node"),
        P("grp", "node"),
    )
    return jax.shard_map(
        body,
        mesh=mesh,
        in_specs=placed,
        out_specs=(P("grp", "node"), P("grp", "node")),
        check_vma=False,
    )
```

```python
import functools

import jax
import jax.numpy as jnp
from jax import lax
from jax.experimental import pallas as pl
from jax.experimental.pallas import tpu as pltpu
from jax.sharding import PartitionSpec as P

CHUNKS = 4
WAYS = 4
CHAINS = 1

relax_factor = 1.9

f32 = jnp.float32
bf16 = jnp.bfloat16


def split(value):
    high = value.astype(bf16).astype(f32)
    return high, value - high


def product(lhs, pair):
    lhs = lhs.astype(bf16)
    return jnp.dot(
        jnp.concatenate([lhs, lhs], axis=1), pair, preferred_element_type=f32
    )


def at8(index):
    return pl.ds(pl.multiple_of(index * 8, 8), 8)


def minus_measured(acc, sino_ref, lo, slices, width, node):
    own = sino_ref.shape[1] // width
    for r in range(own):
        acc[pl.ds((node * own + r) * 8, slices), :] = -sino_ref[
            lo : lo + slices, r * width : (r + 1) * width
        ]


def write_halves(acc, slices, core, half, mine_ref, other_ref):
    for ref, side in ((mine_ref, core), (other_ref, 1 - core)):
        base = side * half * 8
        for s in range(slices):
            ref[s] = (
                acc[pl.ds(base + s, half, stride=8), :]
                + acc[pl.ds(base + s + slices, half, stride=8), :]
            )


def fill_lhs(lhs, p, stride, value, slices):
    high, low = split(value)
    lhs[p * stride : p * stride + slices, :] = high
    lhs[p * stride + slices : p * stride + 2 * slices, :] = low


def first_kernel(
    lo,
    slices,
    rows_hbm,
    patch_hbm,
    count_hbm,
    map_hbm,
    blocks_ref,
    start_hbm,
    sino_hbm,
    mine_ref,
    other_ref,
    col_ref,
    pair_ref,
    turned_ref,
    index_ref,
    rows_ref,
    patch_ref,
    count_ref,
    map_ref,
    start_ref,
    sino_ref,
    stage,
    lhs,
    acc,
    sums,
    sems,
    small_sems,
    *cols,
):
    count_blocks, width, _ = blocks_ref.shape
    total_rows = map_ref.shape[0]
    half = total_rows // 2
    patches = start_ref.shape[1] // width
    node = lax.axis_index("node")
    core = lax.rem(node, 2)
    step = count_blocks // CHUNKS

    def copy(k):
        part = pl.ds(k * step, step)
        return pltpu.make_async_copy(blocks_ref.at[part], stage.at[part], sems.at[k])

    small = [
        pltpu.make_async_copy(src, dst, small_sems.at[i])
        for i, (src, dst) in enumerate(
            (
                (start_hbm, start_ref),
                (sino_hbm, sino_ref),
                (rows_hbm, rows_ref),
                (patch_hbm, patch_ref),
                (count_hbm, count_ref),
                (map_hbm, map_ref),
            )
        )
    ]
    copy(0).start()
    for one in small:
        one.start()
    for k in range(1, CHUNKS):
        copy(k).start()
    acc[...] = jnp.zeros_like(acc)
    sums[...] = jnp.zeros_like(sums)
    for one in cols:
        one[...] = jnp.zeros_like(one)
    lhs[...] = jnp.zeros_like(lhs)
    for one in small:
        one.wait()
    for p in range(patches):
        fill_lhs(lhs, p, 16, start_ref[lo : lo + slices, p * width : (p + 1) * width], slices)
        lhs[p * 16 + 8 : p * 16 + 9, :] = jnp.ones((1, width), f32)
    minus_measured(acc, sino_ref, lo, slices, width, node)
    count = count_ref[0]

    for k in range(CHUNKS):
        copy(k).wait()
        slots = range(k * step, (k + 1) * step)
        places = []
        terms = []
        for j in slots:
            live = j < count
            position = jnp.where(live, map_ref[rows_ref[j]], total_rows)
            patch = jnp.where(live, patch_ref[j], patches)
            index_ref[0, j] = position
            index_ref[1, j] = patch
            places.append(at8(position))
            block = stage[j]
            high = block.astype(bf16)
            low = block - high.astype(f32)
            pair_ref[j, :width, :] = high
            pair_ref[j, width:, :] = low.astype(bf16)
            other = block.T
            high = other.astype(bf16)
            turned = jnp.concatenate([high, (other - high.astype(f32)).astype(bf16)], axis=0)
            turned_ref[j] = turned
            cols[j % WAYS][at8(patch), :] += jnp.sum(block.reshape(width // 8, 8, width), axis=0)
            terms.append(
                product(lhs[pl.ds(pl.multiple_of(patch * 16, 16), 16), :], turned)
            )
        for place, term in zip(places, terms):
            acc[place, :] += term[:8]
            sums[place, :] += term[8:]

    write_halves(acc, slices, core, half, mine_ref, other_ref)
    for ref, side in ((mine_ref, core), (other_ref, 1 - core)):
        ref[slices] = sums[pl.ds(side * half * 8, half, stride=8), :]
    for p in range(patches):
        total = cols[0][at8(p), :]
        for one in cols[1:]:
            total = total + one[at8(p), :]
        total = jnp.sum(total, axis=0, keepdims=True)
        col_ref[p : p + 1, :] = relax_factor / (total + 1.0)


def weigh(slices, mine_ref, other_ref, weight_of, lhs, full, core, half):
    for ref, side in ((mine_ref, core), (other_ref, 1 - core)):
        weight = weight_of(ref, side)
        for s in range(slices):
            value = -weight * ref[s]
            high, low = split(value)
            lhs[pl.ds(side * half * 8 + s, half, stride=8), :] = high
            lhs[pl.ds(side * half * 8 + slices + s, half, stride=8), :] = low
            if full is not None:
                full[s, pl.ds(pl.multiple_of(side * half, 8), half), :] = value


def patch_total(update, p, slices):
    total = update[0][at8(p), :]
    for one in update[1:]:
        total = total + one[at8(p), :]
    return total[:slices] + total[slices : 2 * slices]


def backward(index_ref, pair_ref, lhs, update):
    for one in update:
        one[...] = jnp.zeros_like(one)
    terms = []
    for j in range(pair_ref.shape[0]):
        terms.append(product(lhs[at8(index_ref[0, j]), :], pair_ref[j]))
    for j, term in enumerate(terms):
        update[j % WAYS][at8(index_ref[1, j]), :] += term


def forward(index_ref, turned_ref, lhs, acc):
    terms = []
    for j in range(turned_ref.shape[0]):
        terms.append(product(lhs[at8(index_ref[1, j]), :], turned_ref[j]))
    for j, term in enumerate(terms):
        acc[at8(index_ref[0, j]), :] += term


def middle_kernel(
    lo,
    slices,
    index_ref,
    pair_ref,
    turned_ref,
    mine_ref,
    other_ref,
    col_ref,
    start_ref,
    sino_ref,
    *rest,
):
    given, rest = (rest[:1], rest[1:]) if lo else ((), rest)
    next_mine_ref, next_other_ref, image_ref = rest[:3]
    made, rest = (rest[3:4], rest[4:]) if not lo else ((), rest[3:])
    lhs, acc, image_lhs = rest[:3]
    update = rest[3:]
    width = pair_ref.shape[2]
    half = mine_ref.shape[1]
    patches = start_ref.shape[1] // width
    node = lax.axis_index("node")
    core = lax.rem(node, 2)

    def weight_of(ref, side):
        part = pl.ds(pl.multiple_of(side * half, 8), half)
        if given:
            return given[0][part, :]
        weight = 1.0 / (ref[slices] + 1.0)
        made[0][part, :] = weight
        return weight

    if slices < 4:
        lhs[...] = jnp.zeros_like(lhs)
        image_lhs[...] = jnp.zeros_like(image_lhs)
    lhs[2 * half * 8 :, :] = jnp.zeros((8, width), f32)
    image_lhs[patches * 8 :, :] = jnp.zeros((8, width), f32)
    weigh(slices, mine_ref, other_ref, weight_of, lhs, None, core, half)
    backward(index_ref, pair_ref, lhs, update)
    for p in range(patches):
        total = patch_total(update, p, slices)
        value = (
            start_ref[lo : lo + slices, p * width : (p + 1) * width]
            + col_ref[p : p + 1, :] * total
        )
        image_ref[:, p * width : (p + 1) * width] = value
        fill_lhs(image_lhs, p, 8, value, slices)
    acc[...] = jnp.zeros_like(acc)
    minus_measured(acc, sino_ref, lo, slices, width, node)
    forward(index_ref, turned_ref, image_lhs, acc)
    write_halves(acc, slices, core, half, next_mine_ref, next_other_ref)


def last_kernel(
    lo,
    slices,
    index_ref,
    pair_ref,
    mine_ref,
    other_ref,
    col_ref,
    prior_ref,
    weight_ref,
    *rest,
):
    earlier, rest = (rest[:2], rest[2:]) if lo else ((), rest)
    image_ref, weighted_ref, lhs, full = rest[:4]
    update = rest[4:]
    width = pair_ref.shape[2]
    half = mine_ref.shape[1]
    patches = prior_ref.shape[1] // width
    own = weighted_ref.shape[1] // width
    node = lax.axis_index("node")
    core = lax.rem(node, 2)

    def weight_of(ref, side):
        return weight_ref[pl.ds(pl.multiple_of(side * half, 8), half), :]

    if slices < 4:
        lhs[...] = jnp.zeros_like(lhs)
    if earlier:
        image_ref[:lo, :] = earlier[0][...]
        weighted_ref[:lo, :] = earlier[1][...]
    lhs[2 * half * 8 :, :] = jnp.zeros((8, width), f32)
    weigh(slices, mine_ref, other_ref, weight_of, lhs, full, core, half)
    for s in range(slices):
        for r in range(own):
            weighted_ref[lo + s : lo + s + 1, r * width : (r + 1) * width] = full[
                s, pl.ds(node * own + r, 1), :
            ]
    backward(index_ref, pair_ref, lhs, update)
    for p in range(patches):
        total = patch_total(update, p, slices)
        image_ref[lo : lo + slices, p * width : (p + 1) * width] = (
            prior_ref[:, p * width : (p + 1) * width] + col_ref[p : p + 1, :] * total
        )


def exchange(value, distance, nodes):
    return lax.ppermute(value, "node", [(i, i ^ distance) for i in range(nodes)])


def body(blocks, block_row, block_patch, block_count, row_map, sinogram, start):
    nodes = lax.axis_size("node")
    count_blocks, width, _ = blocks.shape
    all_slices, pixels = start.shape
    slices = all_slices // CHAINS
    patches = pixels // width
    total_rows = row_map.shape[0]
    half = total_rows // 2
    hbm = pl.BlockSpec(memory_space=pltpu.HBM)
    smem = pl.BlockSpec(memory_space=pltpu.SMEM)
    vmem = pl.BlockSpec(memory_space=pltpu.VMEM)
    params = pltpu.CompilerParams(vmem_limit_bytes=28 * 1024 * 1024)
    small_params = pltpu.CompilerParams(vmem_limit_bytes=20 * 1024 * 1024)

    def in_hbm(value):
        return pltpu.with_memory_space_constraint(value, pltpu.HBM)

    def array(*shape):
        return jax.ShapeDtypeStruct(shape, f32)

    distances = [2**k for k in range(1, nodes.bit_length() - 1)]
    swapped = distances[1::-1] + distances[2:]

    def sum_over_nodes(mine, other):
        cut = mine.shape[0] - 2
        values = [
            m + exchange(o, 1, nodes)
            for m, o in ((mine[:cut], other[:cut]), (mine[cut:], other[cut:]))
        ]
        for pair in zip(distances, swapped):
            got = [exchange(v, d, nodes) for v, d in zip(values, pair)]
            values = [v + g for v, g in zip(values, got)]
        others = [exchange(v, 1, nodes) for v in values]
        return jnp.concatenate(values), jnp.concatenate(others)

    acc_shape = pltpu.VMEM((total_rows * 8 + 8, width), f32)
    patch_shape = pltpu.VMEM((patches * 8 + 8, width), f32)

    mine, other, col, pair, turned, index = pl.pallas_call(
        functools.partial(first_kernel, 0, slices),
        out_shape=(
            array(slices + 1, half, width),
            array(slices + 1, half, width),
            array(patches, width),
            pltpu.VMEM((count_blocks, 2 * width, width), bf16),
            pltpu.VMEM((count_blocks, 2 * width, width), bf16),
            pltpu.SMEM((2, count_blocks), jnp.int32),
        ),
        in_specs=[hbm] * 2 + [pl.BlockSpec(memory_space=pl.ANY)] + [hbm] * 4,
        out_specs=(vmem,) * 5 + (smem,),
        scratch_shapes=[
            pltpu.SMEM(block_row.shape, jnp.int32),
            pltpu.SMEM(block_patch.shape, jnp.int32),
            pltpu.SMEM(block_count.shape, jnp.int32),
            pltpu.SMEM(row_map.shape, jnp.int32),
            pltpu.VMEM(start.shape, f32),
            pltpu.VMEM(sinogram.shape, f32),
            pltpu.VMEM(blocks.shape, f32),
            pltpu.VMEM((patches * 16 + 16, width), f32),
            acc_shape,
            acc_shape,
            pltpu.SemaphoreType.DMA((CHUNKS,)),
            pltpu.SemaphoreType.DMA((6,)),
        ]
        + [patch_shape] * WAYS,
        compiler_params=params,
        name="first",
    )(
        in_hbm(block_row),
        in_hbm(block_patch),
        block_count,
        *map(in_hbm, (row_map, blocks, start, sinogram)),
    )

    def held():
        return (
            pltpu.with_memory_space_constraint(index, pltpu.SMEM),
            pltpu.with_memory_space_constraint(pair, pltpu.VMEM),
        )

    terms = [(mine, other)]
    images = []
    weight = None
    for chain in range(CHAINS):
        given = (weight,) if chain else ()
        got = pl.pallas_call(
            functools.partial(middle_kernel, chain * slices, slices),
            out_shape=(
                array(slices, half, width),
                array(slices, half, width),
                array(slices, pixels),
            )
            + (() if chain else (array(total_rows, width),)),
            in_specs=[smem] + [vmem] * (7 + len(given)),
            out_specs=(vmem,) * (3 if chain else 4),
            scratch_shapes=[acc_shape, acc_shape, patch_shape] + [patch_shape] * WAYS,
            compiler_params=small_params,
            name="middle",
        )(
            *held(),
            pltpu.with_memory_space_constraint(turned, pltpu.VMEM),
            *sum_over_nodes(*terms[chain]),
            col, start, sinogram, *given)
        terms[chain] = got[:2]
        images.append(got[2])
        if not chain:
            weight = got[3]
    results = ()
    for chain in range(CHAINS):
        upto = (chain + 1) * slices
        results = pl.pallas_call(
            functools.partial(last_kernel, chain * slices, slices),
            out_shape=(array(upto, pixels), array(upto, sinogram.shape[1])),
            in_specs=[smem] + [vmem] * (6 + len(results)),
            out_specs=(vmem,) * 2,
            scratch_shapes=[
                acc_shape,
                pltpu.VMEM((slices, total_rows, width), f32),
            ]
            + [patch_shape] * WAYS,
            compiler_params=small_params,
            name="last",
        )(*held(), *sum_over_nodes(*terms[chain]), col, images[chain], weight, *results)
    return results


def solution(mesh):
    placed = (
        P(("grp", "node"), None, None),
        P(("grp", "node")),
        P(("grp", "node")),
        P(("grp", "node")),
        P("grp"),
        P("grp", "node"),
        P("grp", "node"),
    )
    return jax.shard_map(
        body,
        mesh=mesh,
        in_specs=placed,
        out_specs=(P("grp", "node"), P("grp", "node")),
        check_vma=False,
    )
```
